768 devices in a mesh: occ: 96 (over z, y_hi, x), vir: 8 (over y_lo, core).
Axes of the slice: x: 4, y: 8 (y_hi: 2, y_lo: 4; y = y_hi * 4 + y_lo), z: 12, core: 2. Of those that a mesh axis runs over, the one named last changes fastest.
Arguments:
- amplitudes: float32 [96, 128, 128, 256], P('occ', 'vir'), may hold values from -6 to 6
- integrals: float32 [384, 256, 128], P('occ', 'vir'), may hold values from -0.09375 to 0.09375
- irrep_occ: int32 [128], replicated, may hold values from 0 to 7
- irrep_j: int32 [3], replicated, may hold values from 0 to 7
- irrep_vir: int32 [256], replicated, may hold values from 0 to 7
- irrep_b: int32 [128], replicated, may hold values from 0 to 7
Outputs:
- cycle_term: float32 [96, 3, 128, 128], P('occ', None, 'vir')
The draws below stay inside these ranges and needn't reach their ends.
Inputs may be any that keep to these rules, and one draw needn't show every extreme that they name: `irrep_occ`: D2h irrep labels. `irrep_j`: D2h irrep labels. `irrep_vir`: D2h irrep labels. `irrep_b`: D2h irrep labels.
All inputs are finite; a program needn't handle non-finite values.
Results may differ from the reference program's by a relative error of at most 0.00007.
Values sent between devices are 32-bit elements; how exact they have to be, the bound alone decides.
No kernel may reach another device: no remote copies, remote signals or barrier semaphores. Data moves between devices by JAX's collectives and lax.ppermute only.
A program may use at most 128 MiB of HBM per device.

```python
import jax
import jax.numpy as jnp
from jax import lax

K = 128
C = 256
A = 128
B = 128
J = 3
I = 96


def touch_ends(values, own_key, smallest, high):
    extent = values.shape
    index_at = [jax.random.randint(jax.random.fold_in(own_key, axis), (), 0, extent[axis]) for axis in range(len(extent))]
    values = values.at[tuple(index_at)].set(smallest)
    longest = extent.index(max(extent))
    index_at[longest] = (index_at[longest] + 1) % extent[longest]
    return values.at[tuple(index_at)].set(high)


def level_of(rng, dims, cuts, least, high):
    loudness = 1.0
    for dim, parts in cuts:
        steps = jax.random.uniform(jax.random.fold_in(jax.random.fold_in(rng, 6), dim), (parts,), jnp.float32, least / len(cuts), high / len(cuts))
        loudness = loudness * jnp.repeat(jnp.exp(steps), dims[dim] // parts).reshape((-1,) + (1,) * (len(dims) - 1 - dim))
    return loudness


def centred(rng, dims, deviation, limit, split=(), held_as=jnp.bfloat16):
    result = deviation * jax.random.normal(rng, dims, jnp.float32)
    if split:
        result = result * level_of(rng, dims, split, -0.22, 0.18)
    return jnp.clip(result, -limit, limit).astype(held_as)


def setup_inputs(seed: int = 0) -> dict:
    seeds = jax.random.split(jax.random.key(seed), 7)
    return {
        "amplitudes": centred(seeds[0], (I, K, A, C), 1.0, 6.0, ((0, 96), (1, 8)), jnp.float32),
        "integrals": centred(seeds[1], (K * J, C, B), (K * C // 8) ** -0.5, 0.09375, ((0, 96), (1, 8)), jnp.float32),
        "irrep_occ": touch_ends(jax.random.randint(seeds[2], (K,), 0, 8), jax.random.fold_in(seeds[2], 1), 0, 7).astype(jnp.int32),
        "irrep_j": jax.random.randint(seeds[3], (J,), 0, 8).astype(jnp.int32),
        "irrep_vir": touch_ends(jax.random.randint(seeds[4], (C,), 0, 8), jax.random.fold_in(seeds[4], 1), 0, 7).astype(jnp.int32),
        "irrep_b": touch_ends(jax.random.randint(seeds[5], (B,), 0, 8), jax.random.fold_in(seeds[5], 1), 0, 7).astype(jnp.int32),
    }


def masked_table(integrals, irrep_occ, irrep_j, irrep_vir, irrep_b):
    table = integrals.reshape(K, J, C, B)
    left_part = jnp.bitwise_xor(irrep_occ[:, None, None, None], irrep_j[None, :, None, None])
    right_part = jnp.bitwise_xor(irrep_vir[None, None, :, None], irrep_b[None, None, None, :])
    parity = jnp.bitwise_xor(left_part, right_part)
    return jnp.where(parity == 0, table, jnp.zeros_like(table))


def reference(amplitudes, integrals, irrep_occ, irrep_j, irrep_vir, irrep_b):
    table = masked_table(integrals, irrep_occ, irrep_j, irrep_vir, irrep_b)

    def one_orbital(orbital_slab):
        return jnp.einsum("kac,kjcb->jab", orbital_slab, table, precision=lax.Precision.HIGHEST)

    return lax.map(one_orbital, amplitudes)
```

```python
import jax
import jax.numpy as jnp
from jax import lax
from jax.experimental import pallas as pl
from jax.experimental.pallas import tpu as pltpu
from jax.sharding import Mesh
from jax.sharding import PartitionSpec as P

J = 3
LANES = 128
ROWS = 4
SLAB = 32
PLACES = 32
HOPS = ("z", "y_hi")
PLANE = ("x", "y_lo", "core")
AXES = ("z", "y_hi", "x", "y_lo", "core")


def columns(row):
    return jnp.broadcast_to(row, (LANES, LANES)).T


def ranks(label_b):
    same = columns(label_b) == label_b
    before = lax.broadcasted_iota(jnp.int32, (LANES, LANES), 0) < lax.broadcasted_iota(jnp.int32, (LANES, LANES), 1)
    return jnp.sum(jnp.where(same & before, 1, 0), axis=0, keepdims=True)


def placing(rank, round_index, part):
    place = rank - round_index * PLACES
    lane = lax.broadcasted_iota(jnp.int32, (LANES, LANES), 0)
    return (lane == place + part * PLACES) & (place >= 0) & (place < PLACES)


def occ_index():
    return (lax.axis_index("z") * 2 + lax.axis_index("y_hi")) * 4 + lax.axis_index("x")


def vir_index():
    return lax.axis_index("y_lo") * 2 + lax.axis_index("core")


def pack_kernel(round_ref, occ_ref, j_ref, vir_ref, b_ref, w_ref, out_ref, rounds_ref, labels):
    label_b = b_ref[...]
    rank = ranks(label_b)
    for half in range(2):
        labels[half * LANES:(half + 1) * LANES, :] = columns(vir_ref[half:half + 1, :])
    start = pl.multiple_of(vir_index() * SLAB, SLAB)
    right = jnp.bitwise_xor(labels[pl.ds(start, SLAB), :], label_b)
    first = occ_index() * ROWS
    total = jnp.zeros((SLAB, LANES), jnp.float32)
    for part in range(ROWS):
        k = lax.div(first + part, J)
        left = jnp.bitwise_xor(occ_ref[k], j_ref[first + part - k * J])
        kept = jnp.where(right == left, w_ref[part], 0.0)
        put = jnp.where(placing(rank, round_ref[0], part), 1.0, 0.0)
        total = total + lax.dot_general(
            kept, put, (((1,), (1,)), ((), ())), precision=lax.Precision.HIGHEST, preferred_element_type=jnp.float32
        )
    out_ref[...] = total
    rounds_ref[0] = lax.div(jnp.max(rank) + PLACES, PLACES)


def halves(values):
    high = values.astype(jnp.bfloat16)
    return high, (values - high.astype(jnp.float32)).astype(jnp.bfloat16)


def multiply_kernel(with_sum, round_ref, occ_ref, j_ref, vir_ref, b_ref, w_ref, t_ref, *rest):
    if with_sum:
        sum_ref, out_ref, w_high, w_low, t_high, t_low = rest
    else:
        out_ref, w_high, w_low, t_high, t_low = rest
    label_b = b_ref[...]
    rank = ranks(label_b)
    label_c = jnp.concatenate([columns(vir_ref[half:half + 1, :]) for half in range(2)], axis=0)
    right = jnp.bitwise_xor(label_c, label_b)
    puts = [jnp.where(placing(rank, round_ref[0], part), 1.0, 0.0).astype(jnp.bfloat16) for part in range(ROWS)]
    split = [halves(w_ref[group]) for group in range(3)]
    first = vir_index() * 16 + lax.axis_index("x") * 4
    for k in range(4):
        for j in range(J):
            group, part = divmod(k * J + j, ROWS)
            keep = right == jnp.bitwise_xor(occ_ref[first + k], j_ref[j])
            for piece, target in zip(split[group], (w_high, w_low)):
                spread = jnp.dot(piece, puts[part], preferred_element_type=jnp.float32)
                target[k * 256:(k + 1) * 256, j * LANES:(j + 1) * LANES] = jnp.where(keep, spread, 0.0).astype(jnp.bfloat16)
        high, low = halves(t_ref[:, k].reshape(4 * LANES, 256))
        t_high[:, k * 256:(k + 1) * 256] = high
        t_low[:, k * 256:(k + 1) * 256] = low
    total = jnp.dot(t_high[...], w_high[...], preferred_element_type=jnp.float32)
    total = total + jnp.dot(t_high[...], w_low[...], preferred_element_type=jnp.float32)
    total = total + jnp.dot(t_low[...], w_high[...], preferred_element_type=jnp.float32)
    for block in range(32):
        for j in range(J):
            piece = total[block * 16:(block + 1) * 16, j * LANES:(j + 1) * LANES]
            if with_sum:
                piece = piece + sum_ref[block, j]
            out_ref[block, j] = piece


SMEM = pl.BlockSpec(memory_space=pltpu.SMEM)
VMEM = pl.BlockSpec(memory_space=pltpu.VMEM)


def pack(round_index, occ, j, vir, b, integrals):
    return pl.pallas_call(
        pack_kernel,
        out_shape=(jax.ShapeDtypeStruct((SLAB, LANES), jnp.float32), jax.ShapeDtypeStruct((1,), jnp.int32)),
        in_specs=[SMEM, SMEM, SMEM, VMEM, VMEM, VMEM],
        out_specs=(VMEM, SMEM),
        scratch_shapes=[pltpu.VMEM((256, LANES), jnp.int32)],
        compiler_params=pltpu.CompilerParams(vmem_limit_bytes=8 << 20),
        name="pack",
    )(round_index, occ, j, vir, b, integrals)


def multiply(round_index, occ, j, vir, b, w, t, total=None):
    with_sum = total is not None
    return pl.pallas_call(
        lambda *refs: multiply_kernel(with_sum, *refs),
        out_shape=jax.ShapeDtypeStruct((32, J, 16, LANES), jnp.float32),
        in_specs=[SMEM, SMEM, SMEM, VMEM, VMEM, VMEM, VMEM] + [VMEM] * with_sum,
        out_specs=VMEM,
        scratch_shapes=[
            pltpu.VMEM((1024, J * LANES), jnp.bfloat16),
            pltpu.VMEM((1024, J * LANES), jnp.bfloat16),
            pltpu.VMEM((512, 1024), jnp.bfloat16),
            pltpu.VMEM((512, 1024), jnp.bfloat16),
        ],
        compiler_params=pltpu.CompilerParams(vmem_limit_bytes=24 << 20),
        cost_estimate=pl.CostEstimate(flops=3 * 2 * 512 * 1024 * 384, bytes_accessed=4 << 20, transcendentals=0),
        name="multiply",
    )(round_index, occ, j, vir, b, w, t, *([total] if with_sum else []))


def owners():
    pairs = []
    for o in range(96):
        for v in range(8):
            place = o % 3 * 8 + v
            pairs.append((o * 8 + v, (place * 4 + o % 12 // 3) * 8 + o // 12))
    return pairs


def local(amplitudes, integrals, irrep_occ, irrep_j, irrep_vir, irrep_b):
    vir, b = irrep_vir.reshape(2, LANES), irrep_b.reshape(1, LANES)
    labels = (irrep_occ, irrep_j, vir, b)

    def column(round_index):
        packed, rounds = pack(round_index, *labels, integrals)
        packed = lax.ppermute(packed, AXES, owners())
        copies = jnp.broadcast_to(packed[None], (24, SLAB, LANES))
        gathered = lax.all_to_all(copies, HOPS, split_axis=0, concat_axis=0, tiled=True)
        return gathered.reshape(3, 256, LANES), rounds

    w, rounds = column(jnp.zeros((1,), jnp.int32))
    t = lax.all_to_all(amplitudes.reshape(4, 4, LANES, 256), "x", split_axis=0, concat_axis=0, tiled=True)
    total = multiply(jnp.zeros((1,), jnp.int32), *labels, w, t)

    def another(state):
        index, total = state
        return index + 1, multiply(index[None], *labels, column(index[None])[0], t, total)

    _, total = lax.while_loop(lambda state: state[0] < rounds[0], another, (jnp.int32(1), total))
    parts = lax.all_to_all(total, PLANE, split_axis=0, concat_axis=0, tiled=True)
    return jnp.sum(parts, axis=0, keepdims=True)


def solution(mesh):
    parts = Mesh(mesh.devices.reshape(12, 2, 4, 4, 2), AXES)
    occ, vir = ("z", "y_hi", "x"), ("y_lo", "core")
    return jax.shard_map(
        local,
        mesh=parts,
        in_specs=(P(occ, vir, None, None), P(occ, vir, None), P(), P(), P(), P()),
        out_specs=P(occ, None, vir, None),
        check_vma=False,
    )
```

```python
import jax
import jax.numpy as jnp
from jax import lax
from jax.experimental import pallas as pl
from jax.experimental.pallas import tpu as pltpu
from jax.sharding import Mesh
from jax.sharding import PartitionSpec as P

J = 3
LANES = 128
ROWS = 4
SLAB = 32
PLACES = 32
HOPS = ("z", "y_hi")
PLANE = ("x", "y_lo", "core")
AXES = ("z", "y_hi", "x", "y_lo", "core")


def columns(row):
    return jnp.broadcast_to(row, (LANES, LANES)).T


def ranks(label_b):
    same = columns(label_b) == label_b
    before = lax.broadcasted_iota(jnp.int32, (LANES, LANES), 0) < lax.broadcasted_iota(jnp.int32, (LANES, LANES), 1)
    return jnp.sum(jnp.where(same & before, 1, 0), axis=0, keepdims=True)


def placing(rank, round_index, part):
    place = rank - round_index * PLACES
    lane = lax.broadcasted_iota(jnp.int32, (LANES, LANES), 0)
    return (lane == place + part * PLACES) & (place >= 0) & (place < PLACES)


def occ_index():
    return (lax.axis_index("z") * 2 + lax.axis_index("y_hi")) * 4 + lax.axis_index("x")


def vir_index():
    return lax.axis_index("y_lo") * 2 + lax.axis_index("core")


def pack_kernel(round_ref, occ_ref, j_ref, vir_ref, b_ref, w_ref, out_ref, rounds_ref, labels):
    label_b = b_ref[...]
    rank = ranks(label_b)
    for half in range(2):
        labels[half * LANES:(half + 1) * LANES, :] = columns(vir_ref[half:half + 1, :])
    start = pl.multiple_of(vir_index() * SLAB, SLAB)
    right = jnp.bitwise_xor(labels[pl.ds(start, SLAB), :], label_b)
    first = occ_index() * ROWS
    total = jnp.zeros((SLAB, LANES), jnp.float32)
    for part in range(ROWS):
        k = lax.div(first + part, J)
        left = jnp.bitwise_xor(occ_ref[k], j_ref[first + part - k * J])
        kept = jnp.where(right == left, w_ref[part], 0.0)
        put = jnp.where(placing(rank, round_ref[0], part), 1.0, 0.0)
        total = total + lax.dot_general(
            kept, put, (((1,), (1,)), ((), ())), precision=lax.Precision.HIGHEST, preferred_element_type=jnp.float32
        )
    out_ref[...] = total
    rounds_ref[0] = lax.div(jnp.max(rank) + PLACES, PLACES)


def halves(values):
    high = values.astype(jnp.bfloat16)
    return high, (values - high.astype(jnp.float32)).astype(jnp.bfloat16)


def multiply_kernel(with_sum, round_ref, occ_ref, j_ref, vir_ref, b_ref, w_ref, *rest):
    t_refs, rest = rest[:4], rest[4:]
    if with_sum:
        sum_ref, out_ref, w_high, w_low, t_high, t_low = rest
    else:
        out_ref, w_high, w_low, t_high, t_low = rest
    label_b = b_ref[...]
    rank = ranks(label_b)
    label_c = jnp.concatenate([columns(vir_ref[half:half + 1, :]) for half in range(2)], axis=0)
    right = jnp.bitwise_xor(label_c, label_b)
    puts = [jnp.where(placing(rank, round_ref[0], part), 1.0, 0.0).astype(jnp.bfloat16) for part in range(ROWS)]
    split = [halves(w_ref[group]) for group in range(3)]
    first = vir_index() * 16 + lax.axis_index("x") * 4
    for k in range(4):
        for j in range(J):
            group, part = divmod(k * J + j, ROWS)
            keep = right == jnp.bitwise_xor(occ_ref[first + k], j_ref[j])
            for piece, target in zip(split[group], (w_high, w_low)):
                spread = jnp.dot(piece, puts[part], preferred_element_type=jnp.float32)
                target[k * 256:(k + 1) * 256, j * LANES:(j + 1) * LANES] = jnp.where(keep, spread, 0.0).astype(jnp.bfloat16)
        for shift, t_ref in enumerate(t_refs):
            high, low = halves(t_ref[k])
            t_high[shift * LANES:(shift + 1) * LANES, k * 256:(k + 1) * 256] = high
            t_low[shift * LANES:(shift + 1) * LANES, k * 256:(k + 1) * 256] = low
    total = jnp.dot(t_high[...], w_high[...], preferred_element_type=jnp.float32)
    total = total + jnp.dot(t_high[...], w_low[...], preferred_element_type=jnp.float32)
    total = total + jnp.dot(t_low[...], w_high[...], preferred_element_type=jnp.float32)
    for shift in range(4):
        source = lax.rem(lax.axis_index("x") + 4 - shift, 4)
        for tile in range(8):
            top = shift * LANES + tile * 16
            for j in range(J):
                piece = total[top:top + 16, j * LANES:(j + 1) * LANES]
                if with_sum:
                    piece = piece + sum_ref[source * 8 + tile, j]
                out_ref[source * 8 + tile, j] = piece


SMEM = pl.BlockSpec(memory_space=pltpu.SMEM)
VMEM = pl.BlockSpec(memory_space=pltpu.VMEM)


def pack(round_index, occ, j, vir, b, integrals):
    return pl.pallas_call(
        pack_kernel,
        out_shape=(jax.ShapeDtypeStruct((SLAB, LANES), jnp.float32), jax.ShapeDtypeStruct((1,), jnp.int32)),
        in_specs=[SMEM, SMEM, SMEM, VMEM, VMEM, VMEM],
        out_specs=(VMEM, SMEM),
        scratch_shapes=[pltpu.VMEM((256, LANES), jnp.int32)],
        compiler_params=pltpu.CompilerParams(vmem_limit_bytes=8 << 20),
        name="pack",
    )(round_index, occ, j, vir, b, integrals)


def multiply(round_index, occ, j, vir, b, w, t, total=None):
    with_sum = total is not None
    return pl.pallas_call(
        lambda *refs: multiply_kernel(with_sum, *refs),
        out_shape=jax.ShapeDtypeStruct((32, J, 16, LANES), jnp.float32),
        in_specs=[SMEM] * 3 + [VMEM] * 7 + [VMEM] * with_sum,
        out_specs=VMEM,
        scratch_shapes=[
            pltpu.VMEM((1024, J * LANES), jnp.bfloat16),
            pltpu.VMEM((1024, J * LANES), jnp.bfloat16),
            pltpu.VMEM((512, 1024), jnp.bfloat16),
            pltpu.VMEM((512, 1024), jnp.bfloat16),
        ],
        compiler_params=pltpu.CompilerParams(vmem_limit_bytes=24 << 20),
        cost_estimate=pl.CostEstimate(flops=3 * 2 * 512 * 1024 * 384, bytes_accessed=4 << 20, transcendentals=0),
        name="multiply",
    )(round_index, occ, j, vir, b, w, *t, *([total] if with_sum else []))


def owners():
    pairs = []
    for o in range(96):
        for v in range(8):
            place = o % 3 * 8 + v
            pairs.append((o * 8 + v, (place * 4 + o % 12 // 3) * 8 + o // 12))
    return pairs


def local(amplitudes, integrals, irrep_occ, irrep_j, irrep_vir, irrep_b):
    vir, b = irrep_vir.reshape(2, LANES), irrep_b.reshape(1, LANES)
    labels = (irrep_occ, irrep_j, vir, b)

    def column(round_index):
        packed, rounds = pack(round_index, *labels, integrals)
        packed = lax.ppermute(packed, AXES, owners())
        copies = jnp.broadcast_to(packed[None], (24, SLAB, LANES))
        gathered = lax.all_to_all(copies, HOPS, split_axis=0, concat_axis=0, tiled=True)
        return gathered.reshape(3, 256, LANES), rounds

    w, rounds = column(jnp.zeros((1,), jnp.int32))
    x = lax.axis_index("x")
    t = []
    for shift in range(4):
        piece = lax.dynamic_slice_in_dim(amplitudes[0], lax.rem(x + shift, 4) * 4, 4)
        t.append(lax.ppermute(piece, "x", [(s, (s + shift) % 4) for s in range(4)]) if shift else piece)
    total = multiply(jnp.zeros((1,), jnp.int32), *labels, w, t)

    def another(state):
        index, total = state
        return index + 1, multiply(index[None], *labels, column(index[None])[0], t, total)

    _, total = lax.while_loop(lambda state: state[0] < rounds[0], another, (jnp.int32(1), total))
    parts = lax.all_to_all(total, PLANE, split_axis=0, concat_axis=0, tiled=True)
    return jnp.sum(parts, axis=0, keepdims=True)


def solution(mesh):
    parts = Mesh(mesh.devices.reshape(12, 2, 4, 4, 2), AXES)
    occ, vir = ("z", "y_hi", "x"), ("y_lo", "core")
    return jax.shard_map(
        local,
        mesh=parts,
        in_specs=(P(occ, vir, None, None), P(occ, vir, None), P(), P(), P(), P()),
        out_specs=P(occ, None, vir, None),
        check_vma=False,
    )
```

```python
import jax
import jax.numpy as jnp
from jax import lax
from jax.experimental import pallas as pl
from jax.experimental.pallas import tpu as pltpu
from jax.sharding import Mesh
from jax.sharding import PartitionSpec as P

J = 3
LANES = 128
ROWS = 4
SLAB = 32
PLACES = 32
HOPS = ("z", "y_hi")
PLANE = ("x", "y_lo", "core")
AXES = ("z", "y_hi", "x", "y_lo", "core")


def columns(row):
    return jnp.broadcast_to(row, (LANES, LANES)).T


def ranks(label_b):
    same = columns(label_b) == label_b
    before = lax.broadcasted_iota(jnp.int32, (LANES, LANES), 0) < lax.broadcasted_iota(jnp.int32, (LANES, LANES), 1)
    return jnp.sum(jnp.where(same & before, 1, 0), axis=0, keepdims=True)


def placing(rank, round_index, part):
    place = rank - round_index * PLACES
    lane = lax.broadcasted_iota(jnp.int32, (LANES, LANES), 0)
    return (lane == place + part * PLACES) & (place >= 0) & (place < PLACES)


def occ_index():
    return (lax.axis_index("z") * 2 + lax.axis_index("y_hi")) * 4 + lax.axis_index("x")


def vir_index():
    return lax.axis_index("y_lo") * 2 + lax.axis_index("core")


def pack_kernel(round_ref, occ_ref, j_ref, vir_ref, b_ref, w_ref, out_ref, rounds_ref, labels):
    label_b = b_ref[...]
    rank = ranks(label_b)
    for half in range(2):
        labels[half * LANES:(half + 1) * LANES, :] = columns(vir_ref[half:half + 1, :])
    start = pl.multiple_of(vir_index() * SLAB, SLAB)
    right = jnp.bitwise_xor(labels[pl.ds(start, SLAB), :], label_b)
    first = occ_index() * ROWS
    total = jnp.zeros((SLAB, LANES), jnp.float32)
    for part in range(ROWS):
        k = lax.div(first + part, J)
        left = jnp.bitwise_xor(occ_ref[k], j_ref[first + part - k * J])
        kept = jnp.where(right == left, w_ref[part], 0.0)
        put = jnp.where(placing(rank, round_ref[0], part), 1.0, 0.0)
        total = total + lax.dot_general(
            kept, put, (((1,), (1,)), ((), ())), precision=lax.Precision.HIGHEST, preferred_element_type=jnp.float32
        )
    out_ref[...] = total
    rounds_ref[0] = lax.div(jnp.max(rank) + PLACES, PLACES)


def halves(values):
    high = values.astype(jnp.bfloat16)
    return high, (values - high.astype(jnp.float32)).astype(jnp.bfloat16)


def multiply_kernel(with_sum, round_ref, occ_ref, j_ref, vir_ref, b_ref, w_ref, *rest):
    t_refs, rest = rest[:4], rest[4:]
    if with_sum:
        sum_ref, out_ref, w_high, w_low, t_high, t_low = rest
    else:
        out_ref, w_high, w_low, t_high, t_low = rest
    label_b = b_ref[...]
    rank = ranks(label_b)
    label_c = jnp.concatenate([columns(vir_ref[half:half + 1, :]) for half in range(2)], axis=0)
    right = jnp.bitwise_xor(label_c, label_b)
    puts = [jnp.where(placing(rank, round_ref[0], part), 1.0, 0.0).astype(jnp.bfloat16) for part in range(ROWS)]
    split = [halves(w_ref[group]) for group in range(3)]
    first = vir_index() * 16 + lax.axis_index("x") * 4
    for k in range(4):
        for j in range(J):
            group, part = divmod(k * J + j, ROWS)
            keep = right == jnp.bitwise_xor(occ_ref[first + k], j_ref[j])
            for piece, target in zip(split[group], (w_high, w_low)):
                spread = jnp.dot(piece, puts[part], preferred_element_type=jnp.float32)
                target[k * 256:(k + 1) * 256, j * LANES:(j + 1) * LANES] = jnp.where(keep, spread, 0.0).astype(jnp.bfloat16)
        for shift, t_ref in enumerate(t_refs):
            high, low = halves(t_ref[k])
            t_high[shift * LANES:(shift + 1) * LANES, k * 256:(k + 1) * 256] = high
            t_low[shift * LANES:(shift + 1) * LANES, k * 256:(k + 1) * 256] = low
    total = jnp.dot(t_high[...], w_high[...], preferred_element_type=jnp.float32)
    total = total + jnp.dot(t_high[...], w_low[...], preferred_element_type=jnp.float32)
    total = total + jnp.dot(t_low[...], w_high[...], preferred_element_type=jnp.float32)
    for shift in range(4):
        source = lax.rem(lax.axis_index("x") + 4 - shift, 4)
        for tile in range(8):
            top = shift * LANES + tile * 16
            for j in range(J):
                piece = total[top:top + 16, j * LANES:(j + 1) * LANES]
                if with_sum:
                    piece = piece + sum_ref[source * 8 + tile, j]
                out_ref[source * 8 + tile, j] = piece


SMEM = pl.BlockSpec(memory_space=pltpu.SMEM)
VMEM = pl.BlockSpec(memory_space=pltpu.VMEM)


def pack(round_index, occ, j, vir, b, integrals):
    return pl.pallas_call(
        pack_kernel,
        out_shape=(jax.ShapeDtypeStruct((SLAB, LANES), jnp.float32), jax.ShapeDtypeStruct((1,), jnp.int32)),
        in_specs=[SMEM, SMEM, SMEM, VMEM, VMEM, VMEM],
        out_specs=(VMEM, SMEM),
        scratch_shapes=[pltpu.VMEM((256, LANES), jnp.int32)],
        compiler_params=pltpu.CompilerParams(vmem_limit_bytes=8 << 20),
        name="pack",
    )(round_index, occ, j, vir, b, integrals)


def multiply(round_index, occ, j, vir, b, w, t, total=None):
    with_sum = total is not None
    return pl.pallas_call(
        lambda *refs: multiply_kernel(with_sum, *refs),
        out_shape=jax.ShapeDtypeStruct((32, J, 16, LANES), jnp.float32),
        in_specs=[SMEM] * 3 + [VMEM] * 7 + [VMEM] * with_sum,
        out_specs=VMEM,
        scratch_shapes=[
            pltpu.VMEM((1024, J * LANES), jnp.bfloat16),
            pltpu.VMEM((1024, J * LANES), jnp.bfloat16),
            pltpu.VMEM((512, 1024), jnp.bfloat16),
            pltpu.VMEM((512, 1024), jnp.bfloat16),
        ],
        compiler_params=pltpu.CompilerParams(vmem_limit_bytes=24 << 20),
        cost_estimate=pl.CostEstimate(flops=3 * 2 * 512 * 1024 * 384, bytes_accessed=4 << 20, transcendentals=0),
        name="multiply",
    )(round_index, occ, j, vir, b, w, *t, *([total] if with_sum else []))


def owners():
    pairs = []
    for o in range(96):
        for v in range(8):
            place = o % 3 * 8 + v
            pairs.append((o * 8 + v, (place * 4 + o % 12 // 3) * 8 + o // 12))
    return pairs


def local(amplitudes, integrals, irrep_occ, irrep_j, irrep_vir, irrep_b):
    vir, b = irrep_vir.reshape(2, LANES), irrep_b.reshape(1, LANES)
    labels = (irrep_occ, irrep_j, vir, b)

    def owned(round_index):
        packed, rounds = pack(round_index, *labels, integrals)
        return lax.ppermute(packed, AXES, owners()), rounds

    def column(packed):
        copies = jnp.broadcast_to(packed[None], (24, SLAB, LANES))
        gathered = lax.all_to_all(copies, HOPS, split_axis=0, concat_axis=0, tiled=True)
        return gathered.reshape(3, 256, LANES)

    x = lax.axis_index("x")
    t = []
    for shift in range(4):
        piece = lax.dynamic_slice_in_dim(amplitudes[0], lax.rem(x + shift, 4) * 4, 4)
        t.append(lax.ppermute(piece, "x", [(s, (s + shift) % 4) for s in range(4)]) if shift else piece)
    packed, rounds = owned(jnp.zeros((1,), jnp.int32))
    packed, t[1], t[3] = lax.optimization_barrier((packed, t[1], t[3]))
    total = multiply(jnp.zeros((1,), jnp.int32), *labels, column(packed), t)

    def another(state):
        index, total = state
        return index + 1, multiply(index[None], *labels, column(owned(index[None])[0]), t, total)

    _, total = lax.while_loop(lambda state: state[0] < rounds[0], another, (jnp.int32(1), total))
    parts = lax.all_to_all(total, PLANE, split_axis=0, concat_axis=0, tiled=True)
    return jnp.sum(parts, axis=0, keepdims=True)


def solution(mesh):
    parts = Mesh(mesh.devices.reshape(12, 2, 4, 4, 2), AXES)
    occ, vir = ("z", "y_hi", "x"), ("y_lo", "core")
    return jax.shard_map(
        local,
        mesh=parts,
        in_specs=(P(occ, vir, None, None), P(occ, vir, None), P(), P(), P(), P()),
        out_specs=P(occ, None, vir, None),
        check_vma=False,
    )
```

```python
import jax
import jax.numpy as jnp
from jax import lax
from jax.experimental import pallas as pl
from jax.experimental.pallas import tpu as pltpu
from jax.sharding import Mesh
from jax.sharding import PartitionSpec as P

J = 3
LANES = 128
ROWS = 4
SLAB = 32
PLACES = 32
HOPS = ("z", "y_hi")
PLANE = ("x", "y_lo")
AXES = ("z", "y_hi", "x", "y_lo", "core")


def columns(row):
    return jnp.broadcast_to(row, (LANES, LANES)).T


def ranks(label_b):
    same = columns(label_b) == label_b
    before = lax.broadcasted_iota(jnp.int32, (LANES, LANES), 0) < lax.broadcasted_iota(jnp.int32, (LANES, LANES), 1)
    return jnp.sum(jnp.where(same & before, 1, 0), axis=0, keepdims=True)


def placing(rank, round_index, part):
    place = rank - round_index * PLACES
    lane = lax.broadcasted_iota(jnp.int32, (LANES, LANES), 0)
    return (lane == place + part * PLACES) & (place >= 0) & (place < PLACES)


def occ_index():
    return (lax.axis_index("z") * 2 + lax.axis_index("y_hi")) * 4 + lax.axis_index("x")


def vir_index():
    return lax.axis_index("y_lo") * 2 + lax.axis_index("core")


def pack_kernel(round_ref, occ_ref, j_ref, vir_ref, b_ref, w_ref, out_ref, rounds_ref, labels):
    label_b = b_ref[...]
    rank = ranks(label_b)
    for half in range(2):
        labels[half * LANES:(half + 1) * LANES, :] = columns(vir_ref[half:half + 1, :])
    start = pl.multiple_of(vir_index() * SLAB, SLAB)
    right = jnp.bitwise_xor(labels[pl.ds(start, SLAB), :], label_b)
    first = occ_index() * ROWS
    total = jnp.zeros((SLAB, LANES), jnp.float32)
    for part in range(ROWS):
        k = lax.div(first + part, J)
        left = jnp.bitwise_xor(occ_ref[k], j_ref[first + part - k * J])
        kept = jnp.where(right == left, w_ref[part], 0.0)
        put = jnp.where(placing(rank, round_ref[0], part), 1.0, 0.0)
        total = total + lax.dot_general(
            kept, put, (((1,), (1,)), ((), ())), precision=lax.Precision.HIGHEST, preferred_element_type=jnp.float32
        )
    out_ref[...] = total
    rounds_ref[0] = lax.div(jnp.max(rank) + PLACES, PLACES)


def halves(values):
    high = values.astype(jnp.bfloat16)
    return high, (values - high.astype(jnp.float32)).astype(jnp.bfloat16)


def multiply_kernel(with_sum, round_ref, occ_ref, j_ref, vir_ref, b_ref, w_ref, *rest):
    t_refs, rest = rest[:4], rest[4:]
    if with_sum:
        sum_ref, out_ref, w_high, w_low, t_high, t_low = rest
    else:
        out_ref, w_high, w_low, t_high, t_low = rest
    label_b = b_ref[...]
    rank = ranks(label_b)
    label_c = jnp.concatenate([columns(vir_ref[half:half + 1, :]) for half in range(2)], axis=0)
    right = jnp.bitwise_xor(label_c, label_b)
    puts = [jnp.where(placing(rank, round_ref[0], part), 1.0, 0.0).astype(jnp.bfloat16) for part in range(ROWS)]
    split = [halves(w_ref[group]) for group in range(3)]
    first = vir_index() * 16 + lax.axis_index("x") * 4
    for k in range(4):
        for j in range(J):
            group, part = divmod(k * J + j, ROWS)
            keep = right == jnp.bitwise_xor(occ_ref[first + k], j_ref[j])
            for piece, target in zip(split[group], (w_high, w_low)):
                spread = jnp.dot(piece, puts[part], preferred_element_type=jnp.float32)
                target[k * 256:(k + 1) * 256, j * LANES:(j + 1) * LANES] = jnp.where(keep, spread, 0.0).astype(jnp.bfloat16)
        for shift, t_ref in enumerate(t_refs):
            high, low = halves(t_ref[k])
            t_high[shift * LANES:(shift + 1) * LANES, k * 256:(k + 1) * 256] = high
            t_low[shift * LANES:(shift + 1) * LANES, k * 256:(k + 1) * 256] = low
    total = jnp.dot(t_high[...], w_high[...], preferred_element_type=jnp.float32)
    total = total + jnp.dot(t_high[...], w_low[...], preferred_element_type=jnp.float32)
    total = total + jnp.dot(t_low[...], w_high[...], preferred_element_type=jnp.float32)
    for shift in range(4):
        source = lax.rem(lax.axis_index("x") + 4 - shift, 4)
        for tile in range(8):
            top = shift * LANES + tile * 16
            for j in range(J):
                piece = total[top:top + 16, j * LANES:(j + 1) * LANES]
                if with_sum:
                    piece = piece + sum_ref[tile % 2, source * 4 + tile // 2, j]
                out_ref[tile % 2, source * 4 + tile // 2, j] = piece


SMEM = pl.BlockSpec(memory_space=pltpu.SMEM)
VMEM = pl.BlockSpec(memory_space=pltpu.VMEM)


def pack(round_index, occ, j, vir, b, integrals):
    return pl.pallas_call(
        pack_kernel,
        out_shape=(jax.ShapeDtypeStruct((SLAB, LANES), jnp.float32), jax.ShapeDtypeStruct((1,), jnp.int32)),
        in_specs=[SMEM, SMEM, SMEM, VMEM, VMEM, VMEM],
        out_specs=(VMEM, SMEM),
        scratch_shapes=[pltpu.VMEM((256, LANES), jnp.int32)],
        compiler_params=pltpu.CompilerParams(vmem_limit_bytes=8 << 20),
        name="pack",
    )(round_index, occ, j, vir, b, integrals)


def multiply(round_index, occ, j, vir, b, w, t, total=None):
    with_sum = total is not None
    return pl.pallas_call(
        lambda *refs: multiply_kernel(with_sum, *refs),
        out_shape=jax.ShapeDtypeStruct((2, 16, J, 16, LANES), jnp.float32),
        in_specs=[SMEM] * 3 + [VMEM] * 7 + [VMEM] * with_sum,
        out_specs=VMEM,
        scratch_shapes=[
            pltpu.VMEM((1024, J * LANES), jnp.bfloat16),
            pltpu.VMEM((1024, J * LANES), jnp.bfloat16),
            pltpu.VMEM((512, 1024), jnp.bfloat16),
            pltpu.VMEM((512, 1024), jnp.bfloat16),
        ],
        compiler_params=pltpu.CompilerParams(vmem_limit_bytes=24 << 20),
        cost_estimate=pl.CostEstimate(flops=3 * 2 * 512 * 1024 * 384, bytes_accessed=4 << 20, transcendentals=0),
        name="multiply",
    )(round_index, occ, j, vir, b, w, *t, *([total] if with_sum else []))


def owners():
    pairs = []
    for o in range(96):
        for v in range(8):
            place = o % 3 * 8 + v
            pairs.append((o * 8 + v, (place * 4 + o % 12 // 3) * 8 + o // 12))
    return pairs


def local(amplitudes, integrals, irrep_occ, irrep_j, irrep_vir, irrep_b):
    vir, b = irrep_vir.reshape(2, LANES), irrep_b.reshape(1, LANES)
    labels = (irrep_occ, irrep_j, vir, b)

    def owned(round_index):
        packed, rounds = pack(round_index, *labels, integrals)
        return lax.ppermute(packed, AXES, owners()), rounds

    def column(packed):
        copies = jnp.broadcast_to(packed[None], (24, SLAB, LANES))
        gathered = lax.all_to_all(copies, HOPS, split_axis=0, concat_axis=0, tiled=True)
        return gathered.reshape(3, 256, LANES)

    x = lax.axis_index("x")
    t = []
    for shift in range(4):
        piece = lax.dynamic_slice_in_dim(amplitudes[0], lax.rem(x + shift, 4) * 4, 4)
        t.append(lax.ppermute(piece, "x", [(s, (s + shift) % 4) for s in range(4)]) if shift else piece)
    packed, rounds = owned(jnp.zeros((1,), jnp.int32))
    packed, t[1], t[3] = lax.optimization_barrier((packed, t[1], t[3]))
    total = multiply(jnp.zeros((1,), jnp.int32), *labels, column(packed), t)

    def another(state):
        index, total = state
        return index + 1, multiply(index[None], *labels, column(owned(index[None])[0]), t, total)

    _, total = lax.while_loop(lambda state: state[0] < rounds[0], another, (jnp.int32(1), total))
    core = lax.axis_index("core")
    given = lax.dynamic_index_in_dim(total, 1 - core, keepdims=False)
    own = lax.dynamic_index_in_dim(total, core, keepdims=False)
    total = own + lax.ppermute(given, "core", [(0, 1), (1, 0)])
    parts = lax.all_to_all(total, PLANE, split_axis=0, concat_axis=0, tiled=True)
    return jnp.sum(parts, axis=0, keepdims=True)


def solution(mesh):
    parts = Mesh(mesh.devices.reshape(12, 2, 4, 4, 2), AXES)
    occ, vir = ("z", "y_hi", "x"), ("y_lo", "core")
    return jax.shard_map(
        local,
        mesh=parts,
        in_specs=(P(occ, vir, None, None), P(occ, vir, None), P(), P(), P(), P()),
        out_specs=P(occ, None, vir, None),
        check_vma=False,
    )
```

```python
import jax
import jax.numpy as jnp
from jax import lax
from jax.experimental import pallas as pl
from jax.experimental.pallas import tpu as pltpu
from jax.sharding import Mesh
from jax.sharding import PartitionSpec as P

J = 3
LANES = 128
ROWS = 4
SLAB = 32
PREPARE_FLOPS = 6_550_000_000
PLACES = 32
HOPS = ("z", "y_hi")
PLANE = ("x", "y_lo")
AXES = ("z", "y_hi", "x", "y_lo", "core")


def columns(row):
    return jnp.broadcast_to(row, (LANES, LANES)).T


def ranks(label_b):
    same = columns(label_b) == label_b
    before = lax.broadcasted_iota(jnp.int32, (LANES, LANES), 0) < lax.broadcasted_iota(jnp.int32, (LANES, LANES), 1)
    return jnp.sum(jnp.where(same & before, 1, 0), axis=0, keepdims=True)


def placing(rank, round_index, part):
    place = rank - round_index * PLACES
    lane = lax.broadcasted_iota(jnp.int32, (LANES, LANES), 0)
    return (lane == place + part * PLACES) & (place >= 0) & (place < PLACES)


def occ_index():
    return (lax.axis_index("z") * 2 + lax.axis_index("y_hi")) * 4 + lax.axis_index("x")


def vir_index():
    return lax.axis_index("y_lo") * 2 + lax.axis_index("core")


def pack_kernel(round_ref, occ_ref, j_ref, vir_ref, b_ref, w_ref, out_ref, rounds_ref, labels):
    label_b = b_ref[...]
    rank = ranks(label_b)
    for half in range(2):
        labels[half * LANES:(half + 1) * LANES, :] = columns(vir_ref[half:half + 1, :])
    start = pl.multiple_of(vir_index() * SLAB, SLAB)
    right = jnp.bitwise_xor(labels[pl.ds(start, SLAB), :], label_b)
    first = occ_index() * ROWS
    total = jnp.zeros((SLAB, LANES), jnp.float32)
    for part in range(ROWS):
        k = lax.div(first + part, J)
        left = jnp.bitwise_xor(occ_ref[k], j_ref[first + part - k * J])
        kept = jnp.where(right == left, w_ref[part], 0.0)
        put = jnp.where(placing(rank, round_ref[0], part), 1.0, 0.0)
        total = total + lax.dot_general(
            kept, put, (((1,), (1,)), ((), ())), precision=lax.Precision.HIGHEST, preferred_element_type=jnp.float32
        )
    out_ref[...] = total
    rounds_ref[0] = lax.div(jnp.max(rank) + PLACES, PLACES)


def halves(values):
    high = values.astype(jnp.bfloat16)
    return high, (values - high.astype(jnp.float32)).astype(jnp.bfloat16)


def prepare_kernel(*refs):
    t_high, t_low = refs[4:]
    for shift, t_ref in enumerate(refs[:4]):
        for k in range(4):
            high, low = halves(t_ref[k])
            t_high[shift * LANES:(shift + 1) * LANES, k * 256:(k + 1) * 256] = high
            t_low[shift * LANES:(shift + 1) * LANES, k * 256:(k + 1) * 256] = low


def multiply_kernel(with_sum, round_ref, occ_ref, j_ref, vir_ref, b_ref, w_ref, t_high, t_low, *rest):
    sums, (own_ref, given_ref, w_high, w_low) = rest[:2 * with_sum], rest[2 * with_sum:]
    label_b = b_ref[...]
    rank = ranks(label_b)
    label_c = jnp.concatenate([columns(vir_ref[half:half + 1, :]) for half in range(2)], axis=0)
    right = jnp.bitwise_xor(label_c, label_b)
    puts = [jnp.where(placing(rank, round_ref[0], part), 1.0, 0.0).astype(jnp.bfloat16) for part in range(ROWS)]
    split = [halves(w_ref[group]) for group in range(3)]
    first = vir_index() * 16 + lax.axis_index("x") * 4
    for k in range(4):
        for j in range(J):
            group, part = divmod(k * J + j, ROWS)
            keep = right == jnp.bitwise_xor(occ_ref[first + k], j_ref[j])
            for piece, target in zip(split[group], (w_high, w_low)):
                spread = jnp.dot(piece, puts[part], preferred_element_type=jnp.float32)
                target[k * 256:(k + 1) * 256, j * LANES:(j + 1) * LANES] = jnp.where(keep, spread, 0.0).astype(jnp.bfloat16)
    total = jnp.dot(t_high[...], w_high[...], preferred_element_type=jnp.float32)
    total = total + jnp.dot(t_high[...], w_low[...], preferred_element_type=jnp.float32)
    total = total + jnp.dot(t_low[...], w_high[...], preferred_element_type=jnp.float32)
    core = lax.axis_index("core")

    def put_out(own, given):
        for shift in range(4):
            source = lax.rem(lax.axis_index("x") + 4 - shift, 4)
            for tile in range(8):
                out_ref = (own, given)[tile % 2]
                top = shift * LANES + tile * 16
                for j in range(J):
                    piece = total[top:top + 16, j * LANES:(j + 1) * LANES]
                    if with_sum:
                        piece = piece + sums[0 if out_ref is own_ref else 1][source * 4 + tile // 2, j]
                    out_ref[source * 4 + tile // 2, j] = piece

    pl.when(core == 0)(lambda: put_out(own_ref, given_ref))
    pl.when(core == 1)(lambda: put_out(given_ref, own_ref))


SMEM = pl.BlockSpec(memory_space=pltpu.SMEM)
VMEM = pl.BlockSpec(memory_space=pltpu.VMEM)


def pack(round_index, occ, j, vir, b, integrals):
    return pl.pallas_call(
        pack_kernel,
        out_shape=(jax.ShapeDtypeStruct((SLAB, LANES), jnp.float32), jax.ShapeDtypeStruct((1,), jnp.int32)),
        in_specs=[SMEM, SMEM, SMEM, VMEM, VMEM, VMEM],
        out_specs=(VMEM, SMEM),
        scratch_shapes=[pltpu.VMEM((256, LANES), jnp.int32)],
        compiler_params=pltpu.CompilerParams(vmem_limit_bytes=8 << 20),
        name="pack",
    )(round_index, occ, j, vir, b, integrals)


def prepare(*t):
    return pl.pallas_call(
        prepare_kernel,
        out_shape=(jax.ShapeDtypeStruct((512, 1024), jnp.bfloat16),) * 2,
        in_specs=[VMEM] * 4,
        out_specs=(VMEM, VMEM),
        compiler_params=pltpu.CompilerParams(vmem_limit_bytes=16 << 20),
        cost_estimate=pl.CostEstimate(flops=PREPARE_FLOPS, bytes_accessed=4 << 20, transcendentals=0),
        name="prepare",
    )(*t)


def multiply(round_index, occ, j, vir, b, w, t_high, t_low, sums=()):
    return pl.pallas_call(
        lambda *refs: multiply_kernel(bool(sums), *refs),
        out_shape=(jax.ShapeDtypeStruct((16, J, 16, LANES), jnp.float32),) * 2,
        in_specs=[SMEM] * 3 + [VMEM] * (5 + len(sums)),
        out_specs=(VMEM, VMEM),
        scratch_shapes=[pltpu.VMEM((1024, J * LANES), jnp.bfloat16)] * 2,
        compiler_params=pltpu.CompilerParams(vmem_limit_bytes=24 << 20),
        cost_estimate=pl.CostEstimate(flops=3 * 2 * 512 * 1024 * 384, bytes_accessed=4 << 20, transcendentals=0),
        name="multiply",
    )(round_index, occ, j, vir, b, w, t_high, t_low, *sums)


def owners():
    pairs = []
    for o in range(96):
        for v in range(8):
            place = o % 3 * 8 + v
            pairs.append((o * 8 + v, (place * 4 + o % 12 // 3) * 8 + o // 12))
    return pairs


def local(amplitudes, integrals, irrep_occ, irrep_j, irrep_vir, irrep_b):
    vir, b = irrep_vir.reshape(2, LANES), irrep_b.reshape(1, LANES)
    labels = (irrep_occ, irrep_j, vir, b)

    def owned(round_index):
        return lax.ppermute(pack(round_index, *labels, integrals)[0], AXES, owners())

    def column(packed):
        copies = jnp.broadcast_to(packed[None], (24, SLAB, LANES))
        gathered = lax.all_to_all(copies, HOPS, split_axis=0, concat_axis=0, tiled=True)
        return gathered.reshape(3, 256, LANES)

    packed, rounds = pack(jnp.zeros((1,), jnp.int32), *labels, integrals)
    packed, amplitudes = lax.optimization_barrier((packed, amplitudes))
    packed = lax.ppermute(packed, AXES, owners())
    x = lax.axis_index("x")
    t = []
    for shift in range(4):
        piece = lax.dynamic_slice_in_dim(amplitudes[0], lax.rem(x + shift, 4) * 4, 4)
        t.append(lax.ppermute(piece, "x", [(s, (s + shift) % 4) for s in range(4)]) if shift else piece)
    t = prepare(*t)
    sums = multiply(jnp.zeros((1,), jnp.int32), *labels, column(packed), *t)

    def another(state):
        index, sums = state
        return index + 1, multiply(index[None], *labels, column(owned(index[None])), *t, sums)

    _, (own, given) = lax.while_loop(lambda state: state[0] < rounds[0], another, (jnp.int32(1), sums))
    total = own + lax.ppermute(given, "core", [(0, 1), (1, 0)])
    parts = lax.all_to_all(total, PLANE, split_axis=0, concat_axis=0, tiled=True)
    return jnp.sum(parts, axis=0, keepdims=True)


def solution(mesh):
    parts = Mesh(mesh.devices.reshape(12, 2, 4, 4, 2), AXES)
    occ, vir = ("z", "y_hi", "x"), ("y_lo", "core")
    return jax.shard_map(
        local,
        mesh=parts,
        in_specs=(P(occ, vir, None, None), P(occ, vir, None), P(), P(), P(), P()),
        out_specs=P(occ, None, vir, None),
        check_vma=False,
    )
```

```python
import jax
import jax.numpy as jnp
from jax import lax
from jax.experimental import pallas as pl
from jax.experimental.pallas import tpu as pltpu
from jax.sharding import Mesh
from jax.sharding import PartitionSpec as P

J = 3
LANES = 128
ROWS = 4
SLAB = 32
PLACES = 32
HOPS = ("z", "y_hi")
PLANE = ("x", "y_lo")
AXES = ("z", "y_hi", "x", "y_lo", "core")


def columns(row):
    return jnp.broadcast_to(row, (LANES, LANES)).T


def ranks(label_b):
    same = columns(label_b) == label_b
    before = lax.broadcasted_iota(jnp.int32, (LANES, LANES), 0) < lax.broadcasted_iota(jnp.int32, (LANES, LANES), 1)
    return jnp.sum(jnp.where(same & before, 1, 0), axis=0, keepdims=True)


def placing(rank, round_index, part):
    place = rank - round_index * PLACES
    lane = lax.broadcasted_iota(jnp.int32, (LANES, LANES), 0)
    return (lane == place + part * PLACES) & (place >= 0) & (place < PLACES)


def occ_index():
    return (lax.axis_index("z") * 2 + lax.axis_index("y_hi")) * 4 + lax.axis_index("x")


def vir_index():
    return lax.axis_index("y_lo") * 2 + lax.axis_index("core")


def pack_kernel(round_ref, occ_ref, j_ref, vir_ref, b_ref, w_ref, out_ref, rounds_ref, labels):
    label_b = b_ref[...]
    rank = ranks(label_b)
    for half in range(2):
        labels[half * LANES:(half + 1) * LANES, :] = columns(vir_ref[half:half + 1, :])
    start = pl.multiple_of(vir_index() * SLAB, SLAB)
    right = jnp.bitwise_xor(labels[pl.ds(start, SLAB), :], label_b)
    first = occ_index() * ROWS
    total = jnp.zeros((SLAB, LANES), jnp.float32)
    for part in range(ROWS):
        k = lax.div(first + part, J)
        left = jnp.bitwise_xor(occ_ref[k], j_ref[first + part - k * J])
        kept = jnp.where(right == left, w_ref[part], 0.0)
        put = jnp.where(placing(rank, round_ref[0], part), 1.0, 0.0)
        total = total + lax.dot_general(
            kept, put, (((1,), (1,)), ((), ())), precision=lax.Precision.HIGHEST, preferred_element_type=jnp.float32
        )
    out_ref[...] = total
    rounds_ref[0] = lax.div(jnp.max(rank) + PLACES, PLACES)


def halves(values):
    high = values.astype(jnp.bfloat16)
    return high, (values - high.astype(jnp.float32)).astype(jnp.bfloat16)


def multiply_kernel(with_sum, round_ref, occ_ref, j_ref, vir_ref, b_ref, w_ref, *rest):
    t_refs, sums, (own_ref, given_ref, w_high, w_low, t_high, t_low) = rest[:4], rest[4:4 + 2 * with_sum], rest[4 + 2 * with_sum:]
    label_b = b_ref[...]
    rank = ranks(label_b)
    label_c = jnp.concatenate([columns(vir_ref[half:half + 1, :]) for half in range(2)], axis=0)
    right = jnp.bitwise_xor(label_c, label_b)
    put = jnp.concatenate(
        [jnp.where(placing(rank, round_ref[0], part), 1.0, 0.0).astype(jnp.bfloat16) for part in range(ROWS)], axis=1
    )
    spreads = [jnp.dot(piece, put, preferred_element_type=jnp.float32) for piece in halves(w_ref[...].reshape(768, LANES))]
    first = vir_index() * 16 + lax.axis_index("x") * 4
    for k in range(4):
        for j in range(J):
            group, part = divmod(k * J + j, ROWS)
            keep = right == jnp.bitwise_xor(occ_ref[first + k], j_ref[j])
            for spread, target in zip(spreads, (w_high, w_low)):
                piece = spread[group * 256:(group + 1) * 256, part * LANES:(part + 1) * LANES]
                target[k * 256:(k + 1) * 256, j * LANES:(j + 1) * LANES] = jnp.where(keep, piece, 0.0).astype(jnp.bfloat16)
        for shift, t_ref in enumerate(t_refs):
            high, low = halves(t_ref[k])
            t_high[shift * LANES:(shift + 1) * LANES, k * 256:(k + 1) * 256] = high
            t_low[shift * LANES:(shift + 1) * LANES, k * 256:(k + 1) * 256] = low
    total = jnp.dot(t_high[...], w_high[...], preferred_element_type=jnp.float32)
    total = total + jnp.dot(t_high[...], w_low[...], preferred_element_type=jnp.float32)
    total = total + jnp.dot(t_low[...], w_high[...], preferred_element_type=jnp.float32)
    core = lax.axis_index("core")

    def put_out(own, given):
        for shift in range(4):
            source = lax.rem(lax.axis_index("x") + 4 - shift, 4)
            for tile in range(8):
                out_ref = (own, given)[tile % 2]
                top = shift * LANES + tile * 16
                for j in range(J):
                    piece = total[top:top + 16, j * LANES:(j + 1) * LANES]
                    if with_sum:
                        piece = piece + sums[0 if out_ref is own_ref else 1][source * 4 + tile // 2, j]
                    out_ref[source * 4 + tile // 2, j] = piece

    pl.when(core == 0)(lambda: put_out(own_ref, given_ref))
    pl.when(core == 1)(lambda: put_out(given_ref, own_ref))


SMEM = pl.BlockSpec(memory_space=pltpu.SMEM)
VMEM = pl.BlockSpec(memory_space=pltpu.VMEM)


def pack(round_index, occ, j, vir, b, integrals):
    return pl.pallas_call(
        pack_kernel,
        out_shape=(jax.ShapeDtypeStruct((SLAB, LANES), jnp.float32), jax.ShapeDtypeStruct((1,), jnp.int32)),
        in_specs=[SMEM, SMEM, SMEM, VMEM, VMEM, VMEM],
        out_specs=(VMEM, SMEM),
        scratch_shapes=[pltpu.VMEM((256, LANES), jnp.int32)],
        compiler_params=pltpu.CompilerParams(vmem_limit_bytes=8 << 20),
        name="pack",
    )(round_index, occ, j, vir, b, integrals)


def multiply(round_index, occ, j, vir, b, w, t, sums=()):
    return pl.pallas_call(
        lambda *refs: multiply_kernel(bool(sums), *refs),
        out_shape=(jax.ShapeDtypeStruct((16, J, 16, LANES), jnp.float32),) * 2,
        in_specs=[SMEM] * 3 + [VMEM] * (7 + len(sums)),
        out_specs=(VMEM, VMEM),
        scratch_shapes=[pltpu.VMEM((1024, J * LANES), jnp.bfloat16)] * 2 + [pltpu.VMEM((512, 1024), jnp.bfloat16)] * 2,
        compiler_params=pltpu.CompilerParams(vmem_limit_bytes=24 << 20),
        cost_estimate=pl.CostEstimate(flops=3 * 2 * 512 * 1024 * 384, bytes_accessed=4 << 20, transcendentals=0),
        name="multiply",
    )(round_index, occ, j, vir, b, w, *t, *sums)


def owners():
    pairs = []
    for o in range(96):
        for v in range(8):
            place = o % 3 * 8 + v
            pairs.append((o * 8 + v, (place * 4 + o % 12 // 3) * 8 + o // 12))
    return pairs


def local(amplitudes, integrals, irrep_occ, irrep_j, irrep_vir, irrep_b):
    vir, b = irrep_vir.reshape(2, LANES), irrep_b.reshape(1, LANES)
    labels = (irrep_occ, irrep_j, vir, b)

    def owned(round_index):
        return lax.ppermute(pack(round_index, *labels, integrals)[0], AXES, owners())

    def column(packed):
        copies = jnp.broadcast_to(packed[None], (24, SLAB, LANES))
        gathered = lax.all_to_all(copies, HOPS, split_axis=0, concat_axis=0, tiled=True)
        return gathered.reshape(3, 256, LANES)

    packed, rounds = pack(jnp.zeros((1,), jnp.int32), *labels, integrals)
    packed_before = packed
    x = lax.axis_index("x")

    def piece(amplitudes, shift):
        return lax.dynamic_slice_in_dim(amplitudes[0], lax.rem(x + shift, 4) * 4, 4)

    def exchanged(piece, shift):
        return lax.ppermute(piece, "x", [(s, (s + shift) % 4) for s in range(4)])

    opposite = exchanged(piece(amplitudes, 2), 2)
    later, packed_before = lax.optimization_barrier((amplitudes, packed_before))
    packed = lax.ppermute(packed_before, AXES, owners())
    t = [piece(later, 0), piece(later, 1), opposite, piece(later, 3)]
    packed, t = lax.optimization_barrier((packed, t))
    t[1], t[3] = exchanged(t[1], 1), exchanged(t[3], 3)
    sums = multiply(jnp.zeros((1,), jnp.int32), *labels, column(packed), t)

    def another(state):
        index, sums = state
        return index + 1, multiply(index[None], *labels, column(owned(index[None])), t, sums)

    _, (own, given) = lax.while_loop(lambda state: state[0] < rounds[0], another, (jnp.int32(1), sums))
    total = own + lax.ppermute(given, "core", [(0, 1), (1, 0)])
    parts = lax.all_to_all(total, PLANE, split_axis=0, concat_axis=0, tiled=True)
    return jnp.sum(parts, axis=0, keepdims=True)


def solution(mesh):
    parts = Mesh(mesh.devices.reshape(12, 2, 4, 4, 2), AXES)
    occ, vir = ("z", "y_hi", "x"), ("y_lo", "core")
    return jax.shard_map(
        local,
        mesh=parts,
        in_specs=(P(occ, vir, None, None), P(occ, vir, None), P(), P(), P(), P()),
        out_specs=P(occ, None, vir, None),
        check_vma=False,
    )
```

```python
import jax
import jax.numpy as jnp
from jax import lax
from jax.experimental import pallas as pl
from jax.experimental.pallas import tpu as pltpu
from jax.sharding import Mesh
from jax.sharding import PartitionSpec as P

J = 3
LANES = 128
ROWS = 4
SLAB = 32
PREPARE_WEIGHT = 6_550_000_000
PLACES = 32
HOPS = ("z", "y_hi")
PLANE = ("x", "y_lo")
AXES = ("z", "y_hi", "x", "y_lo", "core")


def columns(row):
    return jnp.broadcast_to(row, (LANES, LANES)).T


def ranks(label_b):
    same = columns(label_b) == label_b
    before = lax.broadcasted_iota(jnp.int32, (LANES, LANES), 0) < lax.broadcasted_iota(jnp.int32, (LANES, LANES), 1)
    return jnp.sum(jnp.where(same & before, 1, 0), axis=0, keepdims=True)


def placing(rank, round_index, part):
    place = rank - round_index * PLACES
    lane = lax.broadcasted_iota(jnp.int32, (LANES, LANES), 0)
    return (lane == place + part * PLACES) & (place >= 0) & (place < PLACES)


def occ_index():
    return (lax.axis_index("z") * 2 + lax.axis_index("y_hi")) * 4 + lax.axis_index("x")


def vir_index():
    return lax.axis_index("y_lo") * 2 + lax.axis_index("core")


def pack_kernel(round_ref, occ_ref, j_ref, vir_ref, b_ref, w_ref, out_ref, rounds_ref, labels):
    label_b = b_ref[...]
    rank = ranks(label_b)
    for half in range(2):
        labels[half * LANES:(half + 1) * LANES, :] = columns(vir_ref[half:half + 1, :])
    start = pl.multiple_of(vir_index() * SLAB, SLAB)
    right = jnp.bitwise_xor(labels[pl.ds(start, SLAB), :], label_b)
    first = occ_index() * ROWS
    total = jnp.zeros((SLAB, LANES), jnp.float32)
    for part in range(ROWS):
        k = lax.div(first + part, J)
        left = jnp.bitwise_xor(occ_ref[k], j_ref[first + part - k * J])
        kept = jnp.where(right == left, w_ref[part], 0.0)
        put = jnp.where(placing(rank, round_ref[0], part), 1.0, 0.0)
        total = total + lax.dot_general(
            kept, put, (((1,), (1,)), ((), ())), precision=lax.Precision.HIGHEST, preferred_element_type=jnp.float32
        )
    out_ref[...] = total
    rounds_ref[0] = lax.div(jnp.max(rank) + PLACES, PLACES)


def halves(values):
    high = values.astype(jnp.bfloat16)
    return high, (values - high.astype(jnp.float32)).astype(jnp.bfloat16)


def prepare_kernel(t_ref, high_ref, low_ref):
    for k in range(4):
        high_ref[:, k * 256:(k + 1) * 256], low_ref[:, k * 256:(k + 1) * 256] = halves(t_ref[k])


def multiply_kernel(with_sum, round_ref, occ_ref, j_ref, vir_ref, b_ref, w_ref, *rest):
    t_refs, ready, rest = rest[:3], rest[3:5], rest[5:]
    sums, (own_ref, given_ref, w_high, w_low, t_high, t_low) = rest[:2 * with_sum], rest[2 * with_sum:]
    label_b = b_ref[...]
    rank = ranks(label_b)
    label_c = jnp.concatenate([columns(vir_ref[half:half + 1, :]) for half in range(2)], axis=0)
    right = jnp.bitwise_xor(label_c, label_b)
    put = jnp.concatenate(
        [jnp.where(placing(rank, round_ref[0], part), 1.0, 0.0).astype(jnp.bfloat16) for part in range(ROWS)], axis=1
    )
    spreads = [jnp.dot(piece, put, preferred_element_type=jnp.float32) for piece in halves(w_ref[...].reshape(768, LANES))]
    first = vir_index() * 16 + lax.axis_index("x") * 4
    for k in range(4):
        for j in range(J):
            group, part = divmod(k * J + j, ROWS)
            keep = right == jnp.bitwise_xor(occ_ref[first + k], j_ref[j])
            for spread, target in zip(spreads, (w_high, w_low)):
                piece = spread[group * 256:(group + 1) * 256, part * LANES:(part + 1) * LANES]
                target[k * 256:(k + 1) * 256, j * LANES:(j + 1) * LANES] = jnp.where(keep, piece, 0.0).astype(jnp.bfloat16)
        for shift, t_ref in zip((0, 1, 3), t_refs):
            high, low = halves(t_ref[k])
            t_high[shift * LANES:(shift + 1) * LANES, k * 256:(k + 1) * 256] = high
            t_low[shift * LANES:(shift + 1) * LANES, k * 256:(k + 1) * 256] = low
    for ref, target in zip(ready, (t_high, t_low)):
        target[2 * LANES:3 * LANES, :] = ref[...]
    total = jnp.dot(t_high[...], w_high[...], preferred_element_type=jnp.float32)
    total = total + jnp.dot(t_high[...], w_low[...], preferred_element_type=jnp.float32)
    total = total + jnp.dot(t_low[...], w_high[...], preferred_element_type=jnp.float32)
    core = lax.axis_index("core")

    def put_out(own, given):
        for shift in range(4):
            source = lax.rem(lax.axis_index("x") + 4 - shift, 4)
            for tile in range(8):
                out_ref = (own, given)[tile % 2]
                top = shift * LANES + tile * 16
                for j in range(J):
                    piece = total[top:top + 16, j * LANES:(j + 1) * LANES]
                    if with_sum:
                        piece = piece + sums[0 if out_ref is own_ref else 1][source * 4 + tile // 2, j]
                    out_ref[source * 4 + tile // 2, j] = piece

    pl.when(core == 0)(lambda: put_out(own_ref, given_ref))
    pl.when(core == 1)(lambda: put_out(given_ref, own_ref))


SMEM = pl.BlockSpec(memory_space=pltpu.SMEM)
VMEM = pl.BlockSpec(memory_space=pltpu.VMEM)


def pack(round_index, occ, j, vir, b, integrals):
    return pl.pallas_call(
        pack_kernel,
        out_shape=(jax.ShapeDtypeStruct((SLAB, LANES), jnp.float32), jax.ShapeDtypeStruct((1,), jnp.int32)),
        in_specs=[SMEM, SMEM, SMEM, VMEM, VMEM, VMEM],
        out_specs=(VMEM, SMEM),
        scratch_shapes=[pltpu.VMEM((256, LANES), jnp.int32)],
        compiler_params=pltpu.CompilerParams(vmem_limit_bytes=8 << 20),
        name="pack",
    )(round_index, occ, j, vir, b, integrals)


def prepare(t):
    return pl.pallas_call(
        prepare_kernel,
        out_shape=(jax.ShapeDtypeStruct((LANES, 1024), jnp.bfloat16),) * 2,
        in_specs=[VMEM],
        out_specs=(VMEM, VMEM),
        compiler_params=pltpu.CompilerParams(vmem_limit_bytes=8 << 20),
        cost_estimate=pl.CostEstimate(flops=PREPARE_WEIGHT, bytes_accessed=1 << 20, transcendentals=0),
        name="prepare",
    )(t)


def multiply(round_index, occ, j, vir, b, w, t, sums=()):
    return pl.pallas_call(
        lambda *refs: multiply_kernel(bool(sums), *refs),
        out_shape=(jax.ShapeDtypeStruct((16, J, 16, LANES), jnp.float32),) * 2,
        in_specs=[SMEM] * 3 + [VMEM] * (8 + len(sums)),
        out_specs=(VMEM, VMEM),
        scratch_shapes=[pltpu.VMEM((1024, J * LANES), jnp.bfloat16)] * 2 + [pltpu.VMEM((512, 1024), jnp.bfloat16)] * 2,
        compiler_params=pltpu.CompilerParams(vmem_limit_bytes=24 << 20),
        cost_estimate=pl.CostEstimate(flops=3 * 2 * 512 * 1024 * 384, bytes_accessed=4 << 20, transcendentals=0),
        name="multiply",
    )(round_index, occ, j, vir, b, w, *t, *sums)


def owners():
    pairs = []
    for o in range(96):
        for v in range(8):
            place = o % 3 * 8 + v
            pairs.append((o * 8 + v, (place * 4 + o % 12 // 3) * 8 + o // 12))
    return pairs


def local(amplitudes, integrals, irrep_occ, irrep_j, irrep_vir, irrep_b):
    vir, b = irrep_vir.reshape(2, LANES), irrep_b.reshape(1, LANES)
    labels = (irrep_occ, irrep_j, vir, b)

    def owned(round_index):
        return lax.ppermute(pack(round_index, *labels, integrals)[0], AXES, owners())

    def column(packed):
        copies = jnp.broadcast_to(packed[None], (24, SLAB, LANES))
        gathered = lax.all_to_all(copies, HOPS, split_axis=0, concat_axis=0, tiled=True)
        return gathered.reshape(3, 256, LANES)

    packed, rounds = pack(jnp.zeros((1,), jnp.int32), *labels, integrals)
    packed, amplitudes = lax.optimization_barrier((packed, amplitudes))
    packed = lax.ppermute(packed, AXES, owners())
    x = lax.axis_index("x")

    def piece(shift):
        return lax.dynamic_slice_in_dim(amplitudes[0], lax.rem(x + shift, 4) * 4, 4)

    def exchanged(piece, shift):
        return lax.ppermute(piece, "x", [(s, (s + shift) % 4) for s in range(4)])

    opposite = prepare(exchanged(piece(2), 2))
    packed, *near = lax.optimization_barrier((packed, piece(0), piece(1), piece(3)))
    t = [near[0], exchanged(near[1], 1), exchanged(near[2], 3), *opposite]
    sums = multiply(jnp.zeros((1,), jnp.int32), *labels, column(packed), t)

    def another(state):
        index, sums = state
        return index + 1, multiply(index[None], *labels, column(owned(index[None])), t, sums)

    _, (own, given) = lax.while_loop(lambda state: state[0] < rounds[0], another, (jnp.int32(1), sums))
    total = own + lax.ppermute(given, "core", [(0, 1), (1, 0)])
    parts = lax.all_to_all(total, PLANE, split_axis=0, concat_axis=0, tiled=True)
    return jnp.sum(parts, axis=0, keepdims=True)


def solution(mesh):
    parts = Mesh(mesh.devices.reshape(12, 2, 4, 4, 2), AXES)
    occ, vir = ("z", "y_hi", "x"), ("y_lo", "core")
    return jax.shard_map(
        local,
        mesh=parts,
        in_specs=(P(occ, vir, None, None), P(occ, vir, None), P(), P(), P(), P()),
        out_specs=P(occ, None, vir, None),
        check_vma=False,
    )
```

```python
import jax
import jax.numpy as jnp
from jax import lax
from jax.experimental import pallas as pl
from jax.experimental.pallas import tpu as pltpu
from jax.sharding import Mesh
from jax.sharding import PartitionSpec as P

J = 3
LANES = 128
ROWS = 4
SLAB = 32
PREPARE_WEIGHT = 6_550_000_000
PLACES = 32
HOPS = ("z", "y_hi")
PLANE = ("x", "y_lo")
AXES = ("z", "y_hi", "x", "y_lo", "core")


def columns(row):
    return jnp.broadcast_to(row, (LANES, LANES)).T


def ranks(label_b):
    same = columns(label_b) == label_b
    before = lax.broadcasted_iota(jnp.int32, (LANES, LANES), 0) < lax.broadcasted_iota(jnp.int32, (LANES, LANES), 1)
    return jnp.sum(jnp.where(same & before, 1, 0), axis=0, keepdims=True)


def placing(rank, round_index, part):
    place = rank - round_index * PLACES
    lane = lax.broadcasted_iota(jnp.int32, (LANES, LANES), 0)
    return (lane == place + part * PLACES) & (place >= 0) & (place < PLACES)


def occ_index():
    return (lax.axis_index("z") * 2 + lax.axis_index("y_hi")) * 4 + lax.axis_index("x")


def vir_index():
    return lax.axis_index("y_lo") * 2 + lax.axis_index("core")


def halves(values):
    high = values.astype(jnp.bfloat16)
    return high, (values - high.astype(jnp.float32)).astype(jnp.bfloat16)


def pack_kernel(round_ref, occ_ref, j_ref, vir_ref, b_ref, w_ref, out_ref, rounds_ref, labels):
    label_b = b_ref[...]
    rank = ranks(label_b)
    slab = vir_index()
    labels[...] = columns(vir_ref[pl.ds(slab // 4, 1), :])
    start = pl.multiple_of(slab % 4 * SLAB, SLAB)
    right = jnp.bitwise_xor(labels[pl.ds(start, SLAB), :], label_b)
    first = occ_index() * ROWS
    kept, put = [], []
    for part in range(ROWS):
        k = lax.div(first + part, J)
        left = jnp.bitwise_xor(occ_ref[k], j_ref[first + part - k * J])
        kept.append(jnp.where(right == left, w_ref[part], 0.0))
        put.append(jnp.where(placing(rank, round_ref[0], part), 1.0, 0.0).astype(jnp.bfloat16))
    kept, put = jnp.concatenate(kept, axis=1), jnp.concatenate(put, axis=1)
    high = kept.astype(jnp.bfloat16)
    rest = kept - high.astype(jnp.float32)
    middle, low = halves(rest)
    pieces = lax.dot_general(
        jnp.concatenate([high, middle, low], axis=0), put, (((1,), (1,)), ((), ())), preferred_element_type=jnp.float32
    )
    out_ref[...] = (pieces[:SLAB] + pieces[SLAB:2 * SLAB]) + pieces[2 * SLAB:]
    rounds_ref[0] = lax.div(jnp.max(rank) + PLACES, PLACES)


def prepare_kernel(vir_ref, b_ref, t_ref, rank_ref, right_ref, high_ref, low_ref):
    label_b = b_ref[...]
    rank_ref[...] = ranks(label_b)
    for half in range(2):
        label_c = columns(vir_ref[half:half + 1, :])
        right_ref[half * LANES:(half + 1) * LANES, :] = jnp.bitwise_xor(label_c, label_b)
    for k in range(4):
        high_ref[:, k * 256:(k + 1) * 256], low_ref[:, k * 256:(k + 1) * 256] = halves(t_ref[k])


def multiply_kernel(with_sum, round_ref, occ_ref, j_ref, rank_ref, right_ref, w_ref, *rest):
    t_refs, ready, rest = rest[:3], rest[3:5], rest[5:]
    sums, (own_ref, given_ref, w_both, t_high, t_low) = rest[:2 * with_sum], rest[2 * with_sum:]
    rank, right = rank_ref[...], right_ref[...]
    put = jnp.concatenate(
        [jnp.where(placing(rank, round_ref[0], part), 1.0, 0.0).astype(jnp.bfloat16) for part in range(ROWS)], axis=1
    )
    spreads = [jnp.dot(piece, put, preferred_element_type=jnp.float32) for piece in halves(w_ref[...].reshape(768, LANES))]
    first = vir_index() * 16 + lax.axis_index("x") * 4
    for k in range(4):
        for j in range(J):
            group, part = divmod(k * J + j, ROWS)
            keep = right == jnp.bitwise_xor(occ_ref[first + k], j_ref[j])
            for half, spread in enumerate(spreads):
                piece = spread[group * 256:(group + 1) * 256, part * LANES:(part + 1) * LANES]
                column = (half * J + j) * LANES
                w_both[k * 256:(k + 1) * 256, column:column + LANES] = jnp.where(keep, piece, 0.0).astype(jnp.bfloat16)
        for shift, t_ref in zip((0, 1, 3), t_refs):
            high, low = halves(t_ref[k])
            t_high[shift * LANES:(shift + 1) * LANES, k * 256:(k + 1) * 256] = high
            t_low[shift * LANES:(shift + 1) * LANES, k * 256:(k + 1) * 256] = low
    for ref, target in zip(ready, (t_high, t_low)):
        target[2 * LANES:3 * LANES, :] = ref[...]
    both = jnp.dot(t_high[...], w_both[...], preferred_element_type=jnp.float32)
    total = both[:, :J * LANES] + both[:, J * LANES:]
    total = total + jnp.dot(t_low[...], w_both[:, :J * LANES], preferred_element_type=jnp.float32)
    core = lax.axis_index("core")

    def put_out(own, given):
        for shift in range(4):
            source = lax.rem(lax.axis_index("x") + 4 - shift, 4)
            for tile in range(8):
                out_ref = (own, given)[tile % 2]
                top = shift * LANES + tile * 16
                for j in range(J):
                    piece = total[top:top + 16, j * LANES:(j + 1) * LANES]
                    if with_sum:
                        piece = piece + sums[0 if out_ref is own_ref else 1][source * 4 + tile // 2, j]
                    out_ref[source * 4 + tile // 2, j] = piece

    pl.when(core == 0)(lambda: put_out(own_ref, given_ref))
    pl.when(core == 1)(lambda: put_out(given_ref, own_ref))


SMEM = pl.BlockSpec(memory_space=pltpu.SMEM)
VMEM = pl.BlockSpec(memory_space=pltpu.VMEM)


def pack(round_index, occ, j, vir, b, integrals):
    return pl.pallas_call(
        pack_kernel,
        out_shape=(jax.ShapeDtypeStruct((SLAB, LANES), jnp.float32), jax.ShapeDtypeStruct((1,), jnp.int32)),
        in_specs=[SMEM, SMEM, SMEM, VMEM, VMEM, VMEM],
        out_specs=(VMEM, SMEM),
        scratch_shapes=[pltpu.VMEM((LANES, LANES), jnp.int32)],
        compiler_params=pltpu.CompilerParams(vmem_limit_bytes=8 << 20),
        name="pack",
    )(round_index, occ, j, vir, b, integrals)


def prepare(vir, b, t):
    return pl.pallas_call(
        prepare_kernel,
        out_shape=(jax.ShapeDtypeStruct((1, LANES), jnp.int32), jax.ShapeDtypeStruct((256, LANES), jnp.int32))
        + (jax.ShapeDtypeStruct((LANES, 1024), jnp.bfloat16),) * 2,
        in_specs=[VMEM] * 3,
        out_specs=(VMEM,) * 4,
        compiler_params=pltpu.CompilerParams(vmem_limit_bytes=8 << 20),
        cost_estimate=pl.CostEstimate(flops=PREPARE_WEIGHT, bytes_accessed=1 << 20, transcendentals=0),
        name="prepare",
    )(vir, b, t)


def multiply(round_index, occ, j, rank, right, w, t, sums=()):
    return pl.pallas_call(
        lambda *refs: multiply_kernel(bool(sums), *refs),
        out_shape=(jax.ShapeDtypeStruct((16, J, 16, LANES), jnp.float32),) * 2,
        in_specs=[SMEM] * 3 + [VMEM] * (8 + len(sums)),
        out_specs=(VMEM, VMEM),
        scratch_shapes=[pltpu.VMEM((1024, 2 * J * LANES), jnp.bfloat16)] + [pltpu.VMEM((512, 1024), jnp.bfloat16)] * 2,
        compiler_params=pltpu.CompilerParams(vmem_limit_bytes=24 << 20),
        cost_estimate=pl.CostEstimate(flops=3 * 2 * 512 * 1024 * 384, bytes_accessed=4 << 20, transcendentals=0),
        name="multiply",
    )(round_index, occ, j, rank, right, w, *t, *sums)


def owners():
    pairs = []
    for o in range(96):
        for v in range(8):
            place = o % 3 * 8 + v
            pairs.append((o * 8 + v, (place * 4 + o % 12 // 3) * 8 + o // 12))
    return pairs


def local(amplitudes, integrals, irrep_occ, irrep_j, irrep_vir, irrep_b):
    vir, b = irrep_vir.reshape(2, LANES), irrep_b.reshape(1, LANES)
    labels = (irrep_occ, irrep_j, vir, b)

    def owned(round_index):
        return lax.ppermute(pack(round_index, *labels, integrals)[0], AXES, owners())

    def column(packed):
        copies = jnp.broadcast_to(packed[None], (24, SLAB, LANES))
        gathered = lax.all_to_all(copies, HOPS, split_axis=0, concat_axis=0, tiled=True)
        return gathered.reshape(3, 256, LANES)

    packed, rounds = pack(jnp.zeros((1,), jnp.int32), *labels, integrals)
    packed, amplitudes = lax.optimization_barrier((packed, amplitudes))
    packed = lax.ppermute(packed, AXES, owners())
    x = lax.axis_index("x")

    def piece(shift):
        return lax.dynamic_slice_in_dim(amplitudes[0], lax.rem(x + shift, 4) * 4, 4)

    def exchanged(piece, shift):
        return lax.ppermute(piece, "x", [(s, (s + shift) % 4) for s in range(4)])

    rank, right, *opposite = prepare(vir, b, exchanged(piece(2), 2))
    known = (irrep_occ, irrep_j, rank, right)
    packed, *near = lax.optimization_barrier((packed, piece(0), piece(1), piece(3)))
    t = [near[0], exchanged(near[1], 1), exchanged(near[2], 3), *opposite]
    sums = multiply(jnp.zeros((1,), jnp.int32), *known, column(packed), t)

    def another(state):
        index, sums = state
        return index + 1, multiply(index[None], *known, column(owned(index[None])), t, sums)

    _, (own, given) = lax.while_loop(lambda state: state[0] < rounds[0], another, (jnp.int32(1), sums))
    total = own + lax.ppermute(given, "core", [(0, 1), (1, 0)])
    parts = lax.all_to_all(total, PLANE, split_axis=0, concat_axis=0, tiled=True)
    return jnp.sum(parts, axis=0, keepdims=True)


def solution(mesh):
    parts = Mesh(mesh.devices.reshape(12, 2, 4, 4, 2), AXES)
    occ, vir = ("z", "y_hi", "x"), ("y_lo", "core")
    return jax.shard_map(
        local,
        mesh=parts,
        in_specs=(P(occ, vir, None, None), P(occ, vir, None), P(), P(), P(), P()),
        out_specs=P(occ, None, vir, None),
        check_vma=False,
    )
```

```python
import jax
import jax.numpy as jnp
from jax import lax
from jax.experimental import pallas as pl
from jax.experimental.pallas import tpu as pltpu
from jax.sharding import Mesh
from jax.sharding import PartitionSpec as P

J = 3
LANES = 128
ROWS = 4
SLAB = 32
PREPARE_WEIGHT = 6_550_000_000
PLACES = 32
HOPS = ("z", "y_hi")
PLANE = ("x", "y_lo")
AXES = ("z", "y_hi", "x", "y_lo", "core")


def columns(row):
    return jnp.broadcast_to(row, (LANES, LANES)).T


def ranks(label_b):
    same = columns(label_b) == label_b
    before = lax.broadcasted_iota(jnp.int32, (LANES, LANES), 0) < lax.broadcasted_iota(jnp.int32, (LANES, LANES), 1)
    return jnp.sum(jnp.where(same & before, 1, 0), axis=0, keepdims=True)


def placing(rank, round_index, part):
    place = rank - round_index * PLACES
    lane = lax.broadcasted_iota(jnp.int32, (LANES, LANES), 0)
    return (lane == place + part * PLACES) & (place >= 0) & (place < PLACES)


def occ_index():
    return (lax.axis_index("z") * 2 + lax.axis_index("y_hi")) * 4 + lax.axis_index("x")


def vir_index():
    return lax.axis_index("y_lo") * 2 + lax.axis_index("core")


def halves(values):
    high = values.astype(jnp.bfloat16)
    return high, (values - high.astype(jnp.float32)).astype(jnp.bfloat16)


def pack_kernel(round_ref, occ_ref, j_ref, vir_ref, b_ref, w_ref, out_ref, rounds_ref, labels):
    label_b = b_ref[...]
    rank = ranks(label_b)
    slab = vir_index()
    labels[...] = columns(vir_ref[pl.ds(slab // 4, 1), :])
    start = pl.multiple_of(slab % 4 * SLAB, SLAB)
    right = jnp.bitwise_xor(labels[pl.ds(start, SLAB), :], label_b)
    first = occ_index() * ROWS
    kept, put = [], []
    for part in range(ROWS):
        k = lax.div(first + part, J)
        left = jnp.bitwise_xor(occ_ref[k], j_ref[first + part - k * J])
        kept.append(jnp.where(right == left, w_ref[part], 0.0))
        put.append(jnp.where(placing(rank, round_ref[0], part), 1.0, 0.0).astype(jnp.bfloat16))
    kept, put = jnp.concatenate(kept, axis=1), jnp.concatenate(put, axis=1)
    high = kept.astype(jnp.bfloat16)
    rest = kept - high.astype(jnp.float32)
    middle, low = halves(rest)
    pieces = lax.dot_general(
        jnp.concatenate([high, middle, low], axis=0), put, (((1,), (1,)), ((), ())), preferred_element_type=jnp.float32
    )
    out_ref[...] = (pieces[:SLAB] + pieces[SLAB:2 * SLAB]) + pieces[2 * SLAB:]
    rounds_ref[0] = lax.div(jnp.max(rank) + PLACES, PLACES)


def prepare_kernel(vir_ref, b_ref, t_ref, rank_ref, right_ref, high_ref, low_ref):
    label_b = b_ref[...]
    rank_ref[...] = ranks(label_b)
    for half in range(2):
        label_c = columns(vir_ref[half:half + 1, :])
        right_ref[half * LANES:(half + 1) * LANES, :] = jnp.bitwise_xor(label_c, label_b)
    for k in range(4):
        high_ref[:, k * 256:(k + 1) * 256], low_ref[:, k * 256:(k + 1) * 256] = halves(t_ref[k])


def multiply_kernel(with_sum, table_ref, round_ref, occ_ref, j_ref, rank_ref, right_ref, w_ref, *rest):
    t_refs, ready, rest = rest[:3], rest[3:5], rest[5:]
    sums, (own_ref, given_ref, w_both, t_high, t_low) = rest[:2 * with_sum], rest[2 * with_sum:]
    rank, right = rank_ref[...], right_ref[...]
    put = jnp.concatenate(
        [jnp.where(placing(rank, round_ref[0], part), 1.0, 0.0).astype(jnp.bfloat16) for part in range(ROWS)], axis=1
    )
    column = (lax.axis_index("x") * 8 + vir_index()) * 24
    w = jnp.concatenate([w_ref[table_ref[column + block]] for block in range(24)], axis=0)
    spreads = [jnp.dot(piece, put, preferred_element_type=jnp.float32) for piece in halves(w)]
    first = vir_index() * 16 + lax.axis_index("x") * 4
    for k in range(4):
        for j in range(J):
            group, part = divmod(k * J + j, ROWS)
            keep = right == jnp.bitwise_xor(occ_ref[first + k], j_ref[j])
            for half, spread in enumerate(spreads):
                piece = spread[group * 256:(group + 1) * 256, part * LANES:(part + 1) * LANES]
                lane = (half * J + j) * LANES
                w_both[k * 256:(k + 1) * 256, lane:lane + LANES] = jnp.where(keep, piece, 0.0).astype(jnp.bfloat16)
        for shift, t_ref in zip((0, 1, 3), t_refs):
            high, low = halves(t_ref[k])
            t_high[shift * LANES:(shift + 1) * LANES, k * 256:(k + 1) * 256] = high
            t_low[shift * LANES:(shift + 1) * LANES, k * 256:(k + 1) * 256] = low
    for ref, target in zip(ready, (t_high, t_low)):
        target[2 * LANES:3 * LANES, :] = ref[...]
    both = jnp.dot(t_high[...], w_both[...], preferred_element_type=jnp.float32)
    total = both[:, :J * LANES] + both[:, J * LANES:]
    total = total + jnp.dot(t_low[...], w_both[:, :J * LANES], preferred_element_type=jnp.float32)
    core = lax.axis_index("core")

    def put_out(own, given):
        for shift in range(4):
            source = lax.rem(lax.axis_index("x") + 4 - shift, 4)
            for tile in range(8):
                out_ref = (own, given)[tile % 2]
                top = shift * LANES + tile * 16
                for j in range(J):
                    piece = total[top:top + 16, j * LANES:(j + 1) * LANES]
                    if with_sum:
                        piece = piece + sums[0 if out_ref is own_ref else 1][source * 4 + tile // 2, j]
                    out_ref[source * 4 + tile // 2, j] = piece

    pl.when(core == 0)(lambda: put_out(own_ref, given_ref))
    pl.when(core == 1)(lambda: put_out(given_ref, own_ref))


SMEM = pl.BlockSpec(memory_space=pltpu.SMEM)
VMEM = pl.BlockSpec(memory_space=pltpu.VMEM)


def pack(round_index, occ, j, vir, b, integrals):
    return pl.pallas_call(
        pack_kernel,
        out_shape=(jax.ShapeDtypeStruct((SLAB, LANES), jnp.float32), jax.ShapeDtypeStruct((1,), jnp.int32)),
        in_specs=[SMEM, SMEM, SMEM, VMEM, VMEM, VMEM],
        out_specs=(VMEM, SMEM),
        scratch_shapes=[pltpu.VMEM((LANES, LANES), jnp.int32)],
        compiler_params=pltpu.CompilerParams(vmem_limit_bytes=8 << 20),
        name="pack",
    )(round_index, occ, j, vir, b, integrals)


def prepare(vir, b, t):
    return pl.pallas_call(
        prepare_kernel,
        out_shape=(jax.ShapeDtypeStruct((1, LANES), jnp.int32), jax.ShapeDtypeStruct((256, LANES), jnp.int32))
        + (jax.ShapeDtypeStruct((LANES, 1024), jnp.bfloat16),) * 2,
        in_specs=[VMEM] * 3,
        out_specs=(VMEM,) * 4,
        compiler_params=pltpu.CompilerParams(vmem_limit_bytes=8 << 20),
        cost_estimate=pl.CostEstimate(flops=PREPARE_WEIGHT, bytes_accessed=1 << 20, transcendentals=0),
        name="prepare",
    )(vir, b, t)


def multiply(table, round_index, occ, j, rank, right, w, t, sums=()):
    return pl.pallas_call(
        lambda *refs: multiply_kernel(bool(sums), *refs),
        out_shape=(jax.ShapeDtypeStruct((16, J, 16, LANES), jnp.float32),) * 2,
        in_specs=[SMEM] * 4 + [VMEM] * (8 + len(sums)),
        out_specs=(VMEM, VMEM),
        scratch_shapes=[pltpu.VMEM((1024, 2 * J * LANES), jnp.bfloat16)] + [pltpu.VMEM((512, 1024), jnp.bfloat16)] * 2,
        compiler_params=pltpu.CompilerParams(vmem_limit_bytes=24 << 20),
        cost_estimate=pl.CostEstimate(flops=3 * 2 * 512 * 1024 * 384, bytes_accessed=4 << 20, transcendentals=0),
        name="multiply",
    )(table, round_index, occ, j, rank, right, w, *t, *sums)


def hops(source, target):
    (occ, vir), (occ_to, vir_to) = source, target
    spans = (
        (occ % 4 - occ_to % 4, 4),
        (occ // 4 % 2 * 4 + vir // 2 - occ_to // 4 % 2 * 4 - vir_to // 2, 8),
        (occ // 8 - occ_to // 8, 12),
    )
    return sum(min(span % ring, -span % ring) for span, ring in spans)


def matched(costs, limit):
    held = [None] * 24

    def placed(block, seen):
        for place in sorted(range(24), key=lambda place: costs[block][place]):
            if costs[block][place] <= limit and place not in seen:
                seen.add(place)
                if held[place] is None or placed(held[place], seen):
                    held[place] = block
                    return True
        return False

    return held if all(placed(block, set()) for block in range(24)) else None


def owners():
    pairs, table = [], []
    for x in range(4):
        for v in range(8):
            blocks = [(v * 12 + x * 3 + block // 8, block % 8) for block in range(24)]
            costs = [[hops(block, (place * 4 + x, v)) for place in range(24)] for block in blocks]
            held = next(found for found in (matched(costs, limit) for limit in range(20)) if found)
            for place, block in enumerate(held):
                pairs.append((blocks[block][0] * 8 + blocks[block][1], (place * 4 + x) * 8 + v))
            table += [held.index(block) for block in range(24)]
    return pairs, table


def local(amplitudes, integrals, irrep_occ, irrep_j, irrep_vir, irrep_b):
    vir, b = irrep_vir.reshape(2, LANES), irrep_b.reshape(1, LANES)
    pairs, table = owners()
    table = jnp.asarray(table, jnp.int32)
    labels = (irrep_occ, irrep_j, vir, b)

    def owned(round_index):
        return lax.ppermute(pack(round_index, *labels, integrals)[0], AXES, pairs)

    def column(packed):
        copies = jnp.broadcast_to(packed[None], (24, SLAB, LANES))
        gathered = lax.all_to_all(copies, HOPS, split_axis=0, concat_axis=0, tiled=True)
        return gathered

    packed, rounds = pack(jnp.zeros((1,), jnp.int32), *labels, integrals)
    packed, amplitudes = lax.optimization_barrier((packed, amplitudes))
    packed = lax.ppermute(packed, AXES, pairs)
    x = lax.axis_index("x")

    def piece(shift):
        return lax.dynamic_slice_in_dim(amplitudes[0], lax.rem(x + shift, 4) * 4, 4)

    def exchanged(piece, shift):
        return lax.ppermute(piece, "x", [(s, (s + shift) % 4) for s in range(4)])

    rank, right, *opposite = prepare(vir, b, exchanged(piece(2), 2))
    known = (irrep_occ, irrep_j, rank, right)
    packed, *near = lax.optimization_barrier((packed, piece(0), piece(1), piece(3)))
    t = [near[0], exchanged(near[1], 1), exchanged(near[2], 3), *opposite]
    sums = multiply(table, jnp.zeros((1,), jnp.int32), *known, column(packed), t)

    def another(state):
        index, sums = state
        return index + 1, multiply(table, index[None], *known, column(owned(index[None])), t, sums)

    _, (own, given) = lax.while_loop(lambda state: state[0] < rounds[0], another, (jnp.int32(1), sums))
    total = own + lax.ppermute(given, "core", [(0, 1), (1, 0)])
    parts = lax.all_to_all(total, PLANE, split_axis=0, concat_axis=0, tiled=True)
    return jnp.sum(parts, axis=0, keepdims=True)


def solution(mesh):
    parts = Mesh(mesh.devices.reshape(12, 2, 4, 4, 2), AXES)
    occ, vir = ("z", "y_hi", "x"), ("y_lo", "core")
    return jax.shard_map(
        local,
        mesh=parts,
        in_specs=(P(occ, vir, None, None), P(occ, vir, None), P(), P(), P(), P()),
        out_specs=P(occ, None, vir, None),
        check_vma=False,
    )
```

```python
import jax
import jax.numpy as jnp
from jax import lax
from jax.experimental import pallas as pl
from jax.experimental.pallas import tpu as pltpu
from jax.sharding import Mesh
from jax.sharding import PartitionSpec as P

J = 3
LANES = 128
ROWS = 4
SLAB = 32
PREPARE_WEIGHT = 6_550_000_000
PLACES = 32
HOPS = ("z", "y_hi")
PLANE = ("x", "y_lo")
AXES = ("z", "y_hi", "x", "y_lo", "core")


def columns(row):
    return jnp.broadcast_to(row, (LANES, LANES)).T


def ranks(label_b):
    same = columns(label_b) == label_b
    before = lax.broadcasted_iota(jnp.int32, (LANES, LANES), 0) < lax.broadcasted_iota(jnp.int32, (LANES, LANES), 1)
    return jnp.sum(jnp.where(same & before, 1, 0), axis=0, keepdims=True)


def placing(rank, round_index, part):
    place = rank - round_index * PLACES
    lane = lax.broadcasted_iota(jnp.int32, (LANES, LANES), 0)
    return (lane == place + part * PLACES) & (place >= 0) & (place < PLACES)


def occ_index():
    return (lax.axis_index("z") * 2 + lax.axis_index("y_hi")) * 4 + lax.axis_index("x")


def vir_index():
    return lax.axis_index("y_lo") * 2 + lax.axis_index("core")


def halves(values):
    high = values.astype(jnp.bfloat16)
    return high, (values - high.astype(jnp.float32)).astype(jnp.bfloat16)


def pack_kernel(round_ref, occ_ref, j_ref, vir_ref, b_ref, w_ref, out_ref, rounds_ref, labels):
    label_b = b_ref[...]
    rank = ranks(label_b)
    slab = vir_index()
    labels[...] = columns(vir_ref[pl.ds(slab // 4, 1), :])
    start = pl.multiple_of(slab % 4 * SLAB, SLAB)
    right = jnp.bitwise_xor(labels[pl.ds(start, SLAB), :], label_b)
    first = occ_index() * ROWS
    kept, put = [], []
    for part in range(ROWS):
        k = lax.div(first + part, J)
        left = jnp.bitwise_xor(occ_ref[k], j_ref[first + part - k * J])
        kept.append(jnp.where(right == left, w_ref[part], 0.0))
        put.append(jnp.where(placing(rank, round_ref[0], part), 1.0, 0.0).astype(jnp.bfloat16))
    kept, put = jnp.concatenate(kept, axis=1), jnp.concatenate(put, axis=1)
    high = kept.astype(jnp.bfloat16)
    rest = kept - high.astype(jnp.float32)
    middle, low = halves(rest)
    pieces = lax.dot_general(
        jnp.concatenate([high, middle, low], axis=0), put, (((1,), (1,)), ((), ())), preferred_element_type=jnp.float32
    )
    out_ref[...] = (pieces[:SLAB] + pieces[SLAB:2 * SLAB]) + pieces[2 * SLAB:]
    rounds_ref[0] = lax.div(jnp.max(rank) + PLACES, PLACES)


def prepare_kernel(vir_ref, b_ref, near_ref, far_ref, rank_ref, right_ref, high_ref, low_ref):
    label_b = b_ref[...]
    rank_ref[...] = ranks(label_b)
    for half in range(2):
        label_c = columns(vir_ref[half:half + 1, :])
        right_ref[half * LANES:(half + 1) * LANES, :] = jnp.bitwise_xor(label_c, label_b)
    for k in range(4):
        for shift, t_ref in enumerate((near_ref, far_ref)):
            high, low = halves(t_ref[k])
            high_ref[shift * LANES:(shift + 1) * LANES, k * 256:(k + 1) * 256] = high
            low_ref[shift * LANES:(shift + 1) * LANES, k * 256:(k + 1) * 256] = low


def multiply_kernel(with_sum, table_ref, round_ref, occ_ref, j_ref, rank_ref, right_ref, w_ref, *rest):
    t_refs, ready, rest = rest[:2], rest[2:4], rest[4:]
    sums, (own_ref, given_ref, w_both, t_high, t_low) = rest[:2 * with_sum], rest[2 * with_sum:]
    rank, right = rank_ref[...], right_ref[...]
    put = jnp.concatenate(
        [jnp.where(placing(rank, round_ref[0], part), 1.0, 0.0).astype(jnp.bfloat16) for part in range(ROWS)], axis=1
    )
    column = (lax.axis_index("x") * 8 + vir_index()) * 24
    w = jnp.concatenate([w_ref[table_ref[column + block]] for block in range(24)], axis=0)
    spreads = [jnp.dot(piece, put, preferred_element_type=jnp.float32) for piece in halves(w)]
    first = vir_index() * 16 + lax.axis_index("x") * 4
    for k in range(4):
        for j in range(J):
            group, part = divmod(k * J + j, ROWS)
            keep = right == jnp.bitwise_xor(occ_ref[first + k], j_ref[j])
            for half, spread in enumerate(spreads):
                piece = spread[group * 256:(group + 1) * 256, part * LANES:(part + 1) * LANES]
                lane = (half * J + j) * LANES
                w_both[k * 256:(k + 1) * 256, lane:lane + LANES] = jnp.where(keep, piece, 0.0).astype(jnp.bfloat16)
        for shift, t_ref in zip((0, 3), t_refs):
            high, low = halves(t_ref[k])
            t_high[shift * LANES:(shift + 1) * LANES, k * 256:(k + 1) * 256] = high
            t_low[shift * LANES:(shift + 1) * LANES, k * 256:(k + 1) * 256] = low
    for ref, target in zip(ready, (t_high, t_low)):
        target[LANES:3 * LANES, :] = ref[...]
    both = jnp.dot(t_high[...], w_both[...], preferred_element_type=jnp.float32)
    total = both[:, :J * LANES] + both[:, J * LANES:]
    total = total + jnp.dot(t_low[...], w_both[:, :J * LANES], preferred_element_type=jnp.float32)
    core = lax.axis_index("core")

    def put_out(own, given):
        for shift in range(4):
            source = lax.rem(lax.axis_index("x") + 4 - shift, 4)
            for tile in range(8):
                out_ref = (own, given)[tile % 2]
                top = shift * LANES + tile * 16
                for j in range(J):
                    piece = total[top:top + 16, j * LANES:(j + 1) * LANES]
                    if with_sum:
                        piece = piece + sums[0 if out_ref is own_ref else 1][source * 4 + tile // 2, j]
                    out_ref[source * 4 + tile // 2, j] = piece

    pl.when(core == 0)(lambda: put_out(own_ref, given_ref))
    pl.when(core == 1)(lambda: put_out(given_ref, own_ref))


SMEM = pl.BlockSpec(memory_space=pltpu.SMEM)
VMEM = pl.BlockSpec(memory_space=pltpu.VMEM)


def pack(round_index, occ, j, vir, b, integrals):
    return pl.pallas_call(
        pack_kernel,
        out_shape=(jax.ShapeDtypeStruct((SLAB, LANES), jnp.float32), jax.ShapeDtypeStruct((1,), jnp.int32)),
        in_specs=[SMEM, SMEM, SMEM, VMEM, VMEM, VMEM],
        out_specs=(VMEM, SMEM),
        scratch_shapes=[pltpu.VMEM((LANES, LANES), jnp.int32)],
        compiler_params=pltpu.CompilerParams(vmem_limit_bytes=8 << 20),
        name="pack",
    )(round_index, occ, j, vir, b, integrals)


def prepare(vir, b, near, far):
    return pl.pallas_call(
        prepare_kernel,
        out_shape=(jax.ShapeDtypeStruct((1, LANES), jnp.int32), jax.ShapeDtypeStruct((256, LANES), jnp.int32))
        + (jax.ShapeDtypeStruct((2 * LANES, 1024), jnp.bfloat16),) * 2,
        in_specs=[VMEM] * 4,
        out_specs=(VMEM,) * 4,
        compiler_params=pltpu.CompilerParams(vmem_limit_bytes=8 << 20),
        cost_estimate=pl.CostEstimate(flops=PREPARE_WEIGHT, bytes_accessed=1 << 20, transcendentals=0),
        name="prepare",
    )(vir, b, near, far)


def multiply(table, round_index, occ, j, rank, right, w, t, sums=()):
    return pl.pallas_call(
        lambda *refs: multiply_kernel(bool(sums), *refs),
        out_shape=(jax.ShapeDtypeStruct((16, J, 16, LANES), jnp.float32),) * 2,
        in_specs=[SMEM] * 4 + [VMEM] * (7 + len(sums)),
        out_specs=(VMEM, VMEM),
        scratch_shapes=[pltpu.VMEM((1024, 2 * J * LANES), jnp.bfloat16)] + [pltpu.VMEM((512, 1024), jnp.bfloat16)] * 2,
        compiler_params=pltpu.CompilerParams(vmem_limit_bytes=24 << 20),
        cost_estimate=pl.CostEstimate(flops=3 * 2 * 512 * 1024 * 384, bytes_accessed=4 << 20, transcendentals=0),
        name="multiply",
    )(table, round_index, occ, j, rank, right, w, *t, *sums)


def hops(source, target):
    (occ, vir), (occ_to, vir_to) = source, target
    spans = (
        (occ % 4 - occ_to % 4, 4),
        (occ // 4 % 2 * 4 + vir // 2 - occ_to // 4 % 2 * 4 - vir_to // 2, 8),
        (occ // 8 - occ_to // 8, 12),
    )
    return sum(min(span % ring, -span % ring) for span, ring in spans)


def matched(costs, limit):
    held = [None] * 24

    def placed(block, seen):
        for place in sorted(range(24), key=lambda place: costs[block][place]):
            if costs[block][place] <= limit and place not in seen:
                seen.add(place)
                if held[place] is None or placed(held[place], seen):
                    held[place] = block
                    return True
        return False

    return held if all(placed(block, set()) for block in range(24)) else None


def owners():
    pairs, table = [], []
    for x in range(4):
        for v in range(8):
            blocks = [(v * 12 + x * 3 + block // 8, block % 8) for block in range(24)]
            costs = [[hops(block, (place * 4 + x, v)) for place in range(24)] for block in blocks]
            held = next(found for found in (matched(costs, limit) for limit in range(20)) if found)
            for place, block in enumerate(held):
                pairs.append((blocks[block][0] * 8 + blocks[block][1], (place * 4 + x) * 8 + v))
            table += [held.index(block) for block in range(24)]
    return pairs, table


def local(amplitudes, integrals, irrep_occ, irrep_j, irrep_vir, irrep_b):
    vir, b = irrep_vir.reshape(2, LANES), irrep_b.reshape(1, LANES)
    pairs, table = owners()
    table = jnp.asarray(table, jnp.int32)
    labels = (irrep_occ, irrep_j, vir, b)

    def owned(round_index):
        return lax.ppermute(pack(round_index, *labels, integrals)[0], AXES, pairs)

    def column(packed):
        copies = jnp.broadcast_to(packed[None], (24, SLAB, LANES))
        gathered = lax.all_to_all(copies, HOPS, split_axis=0, concat_axis=0, tiled=True)
        return gathered

    packed, rounds = pack(jnp.zeros((1,), jnp.int32), *labels, integrals)
    packed, amplitudes = lax.optimization_barrier((packed, amplitudes))
    packed = lax.ppermute(packed, AXES, pairs)
    x = lax.axis_index("x")

    def piece(shift):
        return lax.dynamic_slice_in_dim(amplitudes[0], lax.rem(x + shift, 4) * 4, 4)

    def exchanged(piece, shift):
        return lax.ppermute(piece, "x", [(s, (s + shift) % 4) for s in range(4)])

    rank, right, *early = prepare(vir, b, exchanged(piece(1), 1), exchanged(piece(2), 2))
    known = (irrep_occ, irrep_j, rank, right)
    packed, *near = lax.optimization_barrier((packed, piece(0), piece(3)))
    t = [near[0], exchanged(near[1], 3), *early]
    sums = multiply(table, jnp.zeros((1,), jnp.int32), *known, column(packed), t)

    def another(state):
        index, sums = state
        return index + 1, multiply(table, index[None], *known, column(owned(index[None])), t, sums)

    _, (own, given) = lax.while_loop(lambda state: state[0] < rounds[0], another, (jnp.int32(1), sums))
    total = own + lax.ppermute(given, "core", [(0, 1), (1, 0)])
    parts = lax.all_to_all(total, PLANE, split_axis=0, concat_axis=0, tiled=True)
    return jnp.sum(parts, axis=0, keepdims=True)


def solution(mesh):
    parts = Mesh(mesh.devices.reshape(12, 2, 4, 4, 2), AXES)
    occ, vir = ("z", "y_hi", "x"), ("y_lo", "core")
    return jax.shard_map(
        local,
        mesh=parts,
        in_specs=(P(occ, vir, None, None), P(occ, vir, None), P(), P(), P(), P()),
        out_specs=P(occ, None, vir, None),
        check_vma=False,
    )
```

```python
import jax
import jax.numpy as jnp
from jax import lax
from jax.experimental import pallas as pl
from jax.experimental.pallas import tpu as pltpu
from jax.sharding import Mesh
from jax.sharding import PartitionSpec as P

J = 3
LANES = 128
ROWS = 4
SLAB = 32
PREPARE_WEIGHT = 6_550_000_000
PLACES = 32
HOPS = ("z", "y_hi")
PLANE = ("x", "y_lo")
AXES = ("z", "y_hi", "x", "y_lo", "core")


def columns(row):
    return jnp.broadcast_to(row, (LANES, LANES)).T


def ranks(label_b):
    same = columns(label_b) == label_b
    before = lax.broadcasted_iota(jnp.int32, (LANES, LANES), 0) < lax.broadcasted_iota(jnp.int32, (LANES, LANES), 1)
    return jnp.sum(jnp.where(same & before, 1, 0), axis=0, keepdims=True)


def placing(rank, round_index, part):
    place = rank - round_index * PLACES
    lane = lax.broadcasted_iota(jnp.int32, (LANES, LANES), 0)
    return (lane == place + part * PLACES) & (place >= 0) & (place < PLACES)


def occ_index():
    return (lax.axis_index("z") * 2 + lax.axis_index("y_hi")) * 4 + lax.axis_index("x")


def vir_index():
    return lax.axis_index("y_lo") * 2 + lax.axis_index("core")


def halves(values):
    high = values.astype(jnp.bfloat16)
    return high, (values - high.astype(jnp.float32)).astype(jnp.bfloat16)


def pack_kernel(round_ref, occ_ref, j_ref, vir_ref, b_ref, w_ref, out_ref, rounds_ref, labels):
    label_b = b_ref[...]
    rank = ranks(label_b)
    slab = vir_index()
    labels[...] = columns(vir_ref[pl.ds(slab // 4, 1), :])
    start = pl.multiple_of(slab % 4 * SLAB, SLAB)
    right = jnp.bitwise_xor(labels[pl.ds(start, SLAB), :], label_b)
    first = occ_index() * ROWS
    kept, put = [], []
    for part in range(ROWS):
        k = lax.div(first + part, J)
        left = jnp.bitwise_xor(occ_ref[k], j_ref[first + part - k * J])
        kept.append(jnp.where(right == left, w_ref[part], 0.0))
        put.append(jnp.where(placing(rank, round_ref[0], part), 1.0, 0.0).astype(jnp.bfloat16))
    kept, put = jnp.concatenate(kept, axis=1), jnp.concatenate(put, axis=1)
    high = kept.astype(jnp.bfloat16)
    rest = kept - high.astype(jnp.float32)
    middle, low = halves(rest)
    pieces = lax.dot_general(
        jnp.concatenate([high, middle, low], axis=0), put, (((1,), (1,)), ((), ())), preferred_element_type=jnp.float32
    )
    out_ref[...] = (pieces[:SLAB] + pieces[SLAB:2 * SLAB]) + pieces[2 * SLAB:]
    rounds_ref[0] = lax.div(jnp.max(rank) + PLACES, PLACES)


def prepare_kernel(vir_ref, b_ref, t_ref, rank_ref, right_ref, high_ref, low_ref):
    label_b = b_ref[...]
    rank_ref[...] = ranks(label_b)
    for half in range(2):
        label_c = columns(vir_ref[half:half + 1, :])
        right_ref[half * LANES:(half + 1) * LANES, :] = jnp.bitwise_xor(label_c, label_b)
    for k in range(4):
        high_ref[:, k * 256:(k + 1) * 256], low_ref[:, k * 256:(k + 1) * 256] = halves(t_ref[k])


def multiply_kernel(with_sum, table_ref, round_ref, occ_ref, j_ref, rank_ref, right_ref, w_ref, *rest):
    t_refs, ready, rest = rest[:3], rest[3:5], rest[5:]
    sums, (own_ref, given_ref, w_both, t_high, t_low) = rest[:2 * with_sum], rest[2 * with_sum:]
    rank, right = rank_ref[...], right_ref[...]
    put = jnp.concatenate(
        [jnp.where(placing(rank, round_ref[0], part), 1.0, 0.0).astype(jnp.bfloat16) for part in range(ROWS)], axis=1
    )
    column = (lax.axis_index("x") * 8 + vir_index()) * 24
    w = jnp.concatenate([w_ref[table_ref[column + block]] for block in range(24)], axis=0)
    spreads = [jnp.dot(piece, put, preferred_element_type=jnp.float32) for piece in halves(w)]
    first = vir_index() * 16 + lax.axis_index("x") * 4
    for k in range(4):
        for j in range(J):
            group, part = divmod(k * J + j, ROWS)
            keep = right == jnp.bitwise_xor(occ_ref[first + k], j_ref[j])
            for half, spread in enumerate(spreads):
                piece = spread[group * 256:(group + 1) * 256, part * LANES:(part + 1) * LANES]
                lane = (half * J + j) * LANES
                w_both[k * 256:(k + 1) * 256, lane:lane + LANES] = jnp.where(keep, piece, 0.0).astype(jnp.bfloat16)
        for shift, t_ref in zip((0, 1, 3), t_refs):
            high, low = halves(t_ref[k])
            t_high[shift * LANES:(shift + 1) * LANES, k * 256:(k + 1) * 256] = high
            t_low[shift * LANES:(shift + 1) * LANES, k * 256:(k + 1) * 256] = low
    for ref, target in zip(ready, (t_high, t_low)):
        target[2 * LANES:3 * LANES, :] = ref[...]
    both = jnp.dot(t_high[...], w_both[...], preferred_element_type=jnp.float32)
    total = both[:, :J * LANES] + both[:, J * LANES:]
    total = total + jnp.dot(t_low[...], w_both[:, :J * LANES], preferred_element_type=jnp.float32)
    core = lax.axis_index("core")

    def put_out(own, given):
        for shift in range(4):
            source = lax.rem(lax.axis_index("x") + 4 - shift, 4)
            for tile in range(8):
                out_ref = (own, given)[tile % 2]
                top = shift * LANES + tile * 16
                for j in range(J):
                    piece = total[top:top + 16, j * LANES:(j + 1) * LANES]
                    if with_sum:
                        piece = piece + sums[0 if out_ref is own_ref else 1][source * 4 + tile // 2, j]
                    out_ref[source * 4 + tile // 2, j] = piece

    pl.when(core == 0)(lambda: put_out(own_ref, given_ref))
    pl.when(core == 1)(lambda: put_out(given_ref, own_ref))


SMEM = pl.BlockSpec(memory_space=pltpu.SMEM)
VMEM = pl.BlockSpec(memory_space=pltpu.VMEM)


def pack(round_index, occ, j, vir, b, integrals):
    return pl.pallas_call(
        pack_kernel,
        out_shape=(jax.ShapeDtypeStruct((SLAB, LANES), jnp.float32), jax.ShapeDtypeStruct((1,), jnp.int32)),
        in_specs=[SMEM, SMEM, SMEM, VMEM, VMEM, VMEM],
        out_specs=(VMEM, SMEM),
        scratch_shapes=[pltpu.VMEM((LANES, LANES), jnp.int32)],
        compiler_params=pltpu.CompilerParams(vmem_limit_bytes=8 << 20),
        name="pack",
    )(round_index, occ, j, vir, b, integrals)


def prepare(vir, b, t):
    return pl.pallas_call(
        prepare_kernel,
        out_shape=(jax.ShapeDtypeStruct((1, LANES), jnp.int32), jax.ShapeDtypeStruct((256, LANES), jnp.int32))
        + (jax.ShapeDtypeStruct((LANES, 1024), jnp.bfloat16),) * 2,
        in_specs=[VMEM] * 3,
        out_specs=(VMEM,) * 4,
        compiler_params=pltpu.CompilerParams(vmem_limit_bytes=8 << 20),
        cost_estimate=pl.CostEstimate(flops=PREPARE_WEIGHT, bytes_accessed=1 << 20, transcendentals=0),
        name="prepare",
    )(vir, b, t)


def multiply(table, round_index, occ, j, rank, right, w, t, sums=()):
    return pl.pallas_call(
        lambda *refs: multiply_kernel(bool(sums), *refs),
        out_shape=(jax.ShapeDtypeStruct((16, J, 16, LANES), jnp.float32),) * 2,
        in_specs=[SMEM] * 4 + [VMEM] * (8 + len(sums)),
        out_specs=(VMEM, VMEM),
        scratch_shapes=[pltpu.VMEM((1024, 2 * J * LANES), jnp.bfloat16)] + [pltpu.VMEM((512, 1024), jnp.bfloat16)] * 2,
        compiler_params=pltpu.CompilerParams(vmem_limit_bytes=24 << 20),
        cost_estimate=pl.CostEstimate(flops=3 * 2 * 512 * 1024 * 384, bytes_accessed=4 << 20, transcendentals=0),
        name="multiply",
    )(table, round_index, occ, j, rank, right, w, *t, *sums)


def hops(source, target):
    (occ, vir), (occ_to, vir_to) = source, target
    spans = (
        (occ % 4 - occ_to % 4, 4),
        (occ // 4 % 2 * 4 + vir // 2 - occ_to // 4 % 2 * 4 - vir_to // 2, 8),
        (occ // 8 - occ_to // 8, 12),
    )
    return sum(min(span % ring, -span % ring) for span, ring in spans)


def matched(costs, limit):
    held = [None] * 24

    def placed(block, seen):
        for place in sorted(range(24), key=lambda place: costs[block][place]):
            if costs[block][place] <= limit and place not in seen:
                seen.add(place)
                if held[place] is None or placed(held[place], seen):
                    held[place] = block
                    return True
        return False

    return held if all(placed(block, set()) for block in range(24)) else None


def owners():
    pairs, table = [], []
    for x in range(4):
        for v in range(8):
            blocks = [(v * 12 + x * 3 + block // 8, block % 8) for block in range(24)]
            costs = [[hops(block, (place * 4 + x, v)) for place in range(24)] for block in blocks]
            held = next(found for found in (matched(costs, limit) for limit in range(20)) if found)
            for place, block in enumerate(held):
                pairs.append((blocks[block][0] * 8 + blocks[block][1], (place * 4 + x) * 8 + v))
            table += [held.index(block) for block in range(24)]
    return pairs, table


def local(amplitudes, integrals, irrep_occ, irrep_j, irrep_vir, irrep_b):
    vir, b = irrep_vir.reshape(2, LANES), irrep_b.reshape(1, LANES)
    pairs, table = owners()
    table = jnp.asarray(table, jnp.int32)
    labels = (irrep_occ, irrep_j, vir, b)

    def owned(round_index):
        return lax.ppermute(pack(round_index, *labels, integrals)[0], AXES, pairs)

    def column(packed):
        copies = jnp.broadcast_to(packed[None], (24, SLAB, LANES))
        gathered = lax.all_to_all(copies, HOPS, split_axis=0, concat_axis=0, tiled=True)
        return gathered

    packed, rounds = pack(jnp.zeros((1,), jnp.int32), *labels, integrals)
    packed, amplitudes = lax.optimization_barrier((packed, amplitudes))
    packed = lax.ppermute(packed, AXES, pairs)
    x = lax.axis_index("x")

    def piece(amplitudes, shift):
        return lax.dynamic_slice_in_dim(amplitudes[0], lax.rem(x + shift, 4) * 4, 4)

    def exchanged(piece, shift):
        return lax.ppermute(piece, "x", [(s, (s + shift) % 4) for s in range(4)])

    far, amplitudes = lax.optimization_barrier((piece(amplitudes, 2), amplitudes))
    rank, right, *opposite = prepare(vir, b, exchanged(far, 2))
    known = (irrep_occ, irrep_j, rank, right)
    packed, *near = lax.optimization_barrier((packed, *(piece(amplitudes, shift) for shift in (0, 1, 3))))
    t = [near[0], exchanged(near[1], 1), exchanged(near[2], 3), *opposite]
    sums = multiply(table, jnp.zeros((1,), jnp.int32), *known, column(packed), t)

    def another(state):
        index, sums = state
        return index + 1, multiply(table, index[None], *known, column(owned(index[None])), t, sums)

    _, (own, given) = lax.while_loop(lambda state: state[0] < rounds[0], another, (jnp.int32(1), sums))
    total = own + lax.ppermute(given, "core", [(0, 1), (1, 0)])
    parts = lax.all_to_all(total, PLANE, split_axis=0, concat_axis=0, tiled=True)
    return jnp.sum(parts, axis=0, keepdims=True)


def solution(mesh):
    parts = Mesh(mesh.devices.reshape(12, 2, 4, 4, 2), AXES)
    occ, vir = ("z", "y_hi", "x"), ("y_lo", "core")
    return jax.shard_map(
        local,
        mesh=parts,
        in_specs=(P(occ, vir, None, None), P(occ, vir, None), P(), P(), P(), P()),
        out_specs=P(occ, None, vir, None),
        check_vma=False,
    )
```

```python
import itertools

import jax
import jax.numpy as jnp
from jax import lax
from jax.experimental import pallas as pl
from jax.experimental.pallas import tpu as pltpu
from jax.sharding import Mesh
from jax.sharding import PartitionSpec as P

J = 3
LANES = 128
ROWS = 4
SLAB = 32
PREPARE_WEIGHT = 6_550_000_000
PLACES = 32
HOPS = ("z", "y_hi")
PLANE = ("x", "y_lo")
AXES = ("z", "y_hi", "x", "y_lo", "core")


def columns(row):
    return jnp.broadcast_to(row, (LANES, LANES)).T


def ranks(label_b):
    same = columns(label_b) == label_b
    before = lax.broadcasted_iota(jnp.int32, (LANES, LANES), 0) < lax.broadcasted_iota(jnp.int32, (LANES, LANES), 1)
    return jnp.sum(jnp.where(same & before, 1, 0), axis=0, keepdims=True)


def placing(rank, round_index, part):
    place = rank - round_index * PLACES
    lane = lax.broadcasted_iota(jnp.int32, (LANES, LANES), 0)
    return (lane == place + part * PLACES) & (place >= 0) & (place < PLACES)


def occ_index():
    return (lax.axis_index("z") * 2 + lax.axis_index("y_hi")) * 4 + lax.axis_index("x")


def vir_index():
    return lax.axis_index("y_lo") * 2 + lax.axis_index("core")


def halves(values):
    high = values.astype(jnp.bfloat16)
    return high, (values - high.astype(jnp.float32)).astype(jnp.bfloat16)


def pack_kernel(round_ref, occ_ref, j_ref, vir_ref, b_ref, w_ref, out_ref, rounds_ref, labels):
    label_b = b_ref[...]
    rank = ranks(label_b)
    slab = vir_index()
    labels[...] = columns(vir_ref[pl.ds(slab // 4, 1), :])
    start = pl.multiple_of(slab % 4 * SLAB, SLAB)
    right = jnp.bitwise_xor(labels[pl.ds(start, SLAB), :], label_b)
    first = occ_index() * ROWS
    kept, put = [], []
    for part in range(ROWS):
        k = lax.div(first + part, J)
        left = jnp.bitwise_xor(occ_ref[k], j_ref[first + part - k * J])
        kept.append(jnp.where(right == left, w_ref[part], 0.0))
        put.append(jnp.where(placing(rank, round_ref[0], part), 1.0, 0.0).astype(jnp.bfloat16))
    kept, put = jnp.concatenate(kept, axis=1), jnp.concatenate(put, axis=1)
    high = kept.astype(jnp.bfloat16)
    rest = kept - high.astype(jnp.float32)
    middle, low = halves(rest)
    pieces = lax.dot_general(
        jnp.concatenate([high, middle, low], axis=0), put, (((1,), (1,)), ((), ())), preferred_element_type=jnp.float32
    )
    out_ref[...] = (pieces[:SLAB] + pieces[SLAB:2 * SLAB]) + pieces[2 * SLAB:]
    rounds_ref[0] = lax.div(jnp.max(rank) + PLACES, PLACES)


def prepare_kernel(vir_ref, b_ref, t_ref, rank_ref, right_ref, high_ref, low_ref):
    label_b = b_ref[...]
    rank_ref[...] = ranks(label_b)
    for half in range(2):
        label_c = columns(vir_ref[half:half + 1, :])
        right_ref[half * LANES:(half + 1) * LANES, :] = jnp.bitwise_xor(label_c, label_b)
    for k in range(4):
        high_ref[:, k * 256:(k + 1) * 256], low_ref[:, k * 256:(k + 1) * 256] = halves(t_ref[k])


def multiply_kernel(with_sum, table_ref, round_ref, occ_ref, j_ref, rank_ref, right_ref, w_ref, *rest):
    t_refs, ready, rest = rest[:3], rest[3:5], rest[5:]
    sums, (own_ref, given_ref, w_both, t_high, t_low) = rest[:2 * with_sum], rest[2 * with_sum:]
    rank, right = rank_ref[...], right_ref[...]
    put = jnp.concatenate(
        [jnp.where(placing(rank, round_ref[0], part), 1.0, 0.0).astype(jnp.bfloat16) for part in range(ROWS)], axis=1
    )
    column = (lax.axis_index("x") * 8 + vir_index()) * 24
    w = jnp.concatenate([w_ref[table_ref[column + block]] for block in range(24)], axis=0)
    spreads = [jnp.dot(piece, put, preferred_element_type=jnp.float32) for piece in halves(w)]
    first = vir_index() * 16 + lax.axis_index("x") * 4
    for k in range(4):
        for j in range(J):
            group, part = divmod(k * J + j, ROWS)
            keep = right == jnp.bitwise_xor(occ_ref[first + k], j_ref[j])
            for half, spread in enumerate(spreads):
                piece = spread[group * 256:(group + 1) * 256, part * LANES:(part + 1) * LANES]
                lane = (half * J + j) * LANES
                w_both[k * 256:(k + 1) * 256, lane:lane + LANES] = jnp.where(keep, piece, 0.0).astype(jnp.bfloat16)
        for shift, t_ref in zip((0, 1, 3), t_refs):
            high, low = halves(t_ref[k])
            t_high[shift * LANES:(shift + 1) * LANES, k * 256:(k + 1) * 256] = high
            t_low[shift * LANES:(shift + 1) * LANES, k * 256:(k + 1) * 256] = low
    for ref, target in zip(ready, (t_high, t_low)):
        target[2 * LANES:3 * LANES, :] = ref[...]
    both = jnp.dot(t_high[...], w_both[...], preferred_element_type=jnp.float32)
    total = both[:, :J * LANES] + both[:, J * LANES:]
    total = total + jnp.dot(t_low[...], w_both[:, :J * LANES], preferred_element_type=jnp.float32)
    core = lax.axis_index("core")

    def put_out(own, given):
        for shift in range(4):
            source = lax.rem(lax.axis_index("x") + 4 - shift, 4)
            for tile in range(8):
                out_ref = (own, given)[tile % 2]
                top = shift * LANES + tile * 16
                for j in range(J):
                    piece = total[top:top + 16, j * LANES:(j + 1) * LANES]
                    if with_sum:
                        piece = piece + sums[0 if out_ref is own_ref else 1][source * 4 + tile // 2, j]
                    out_ref[source * 4 + tile // 2, j] = piece

    pl.when(core == 0)(lambda: put_out(own_ref, given_ref))
    pl.when(core == 1)(lambda: put_out(given_ref, own_ref))


SMEM = pl.BlockSpec(memory_space=pltpu.SMEM)
VMEM = pl.BlockSpec(memory_space=pltpu.VMEM)


def pack(round_index, occ, j, vir, b, integrals):
    return pl.pallas_call(
        pack_kernel,
        out_shape=(jax.ShapeDtypeStruct((SLAB, LANES), jnp.float32), jax.ShapeDtypeStruct((1,), jnp.int32)),
        in_specs=[SMEM, SMEM, SMEM, VMEM, VMEM, VMEM],
        out_specs=(VMEM, SMEM),
        scratch_shapes=[pltpu.VMEM((LANES, LANES), jnp.int32)],
        compiler_params=pltpu.CompilerParams(vmem_limit_bytes=8 << 20),
        name="pack",
    )(round_index, occ, j, vir, b, integrals)


def prepare(vir, b, t):
    return pl.pallas_call(
        prepare_kernel,
        out_shape=(jax.ShapeDtypeStruct((1, LANES), jnp.int32), jax.ShapeDtypeStruct((256, LANES), jnp.int32))
        + (jax.ShapeDtypeStruct((LANES, 1024), jnp.bfloat16),) * 2,
        in_specs=[VMEM] * 3,
        out_specs=(VMEM,) * 4,
        compiler_params=pltpu.CompilerParams(vmem_limit_bytes=8 << 20),
        cost_estimate=pl.CostEstimate(flops=PREPARE_WEIGHT, bytes_accessed=1 << 20, transcendentals=0),
        name="prepare",
    )(vir, b, t)


def multiply(table, round_index, occ, j, rank, right, w, t, sums=()):
    return pl.pallas_call(
        lambda *refs: multiply_kernel(bool(sums), *refs),
        out_shape=(jax.ShapeDtypeStruct((16, J, 16, LANES), jnp.float32),) * 2,
        in_specs=[SMEM] * 4 + [VMEM] * (8 + len(sums)),
        out_specs=(VMEM, VMEM),
        scratch_shapes=[pltpu.VMEM((1024, 2 * J * LANES), jnp.bfloat16)] + [pltpu.VMEM((512, 1024), jnp.bfloat16)] * 2,
        compiler_params=pltpu.CompilerParams(vmem_limit_bytes=24 << 20),
        cost_estimate=pl.CostEstimate(flops=3 * 2 * 512 * 1024 * 384, bytes_accessed=4 << 20, transcendentals=0),
        name="multiply",
    )(table, round_index, occ, j, rank, right, w, *t, *sums)


def hops(source, target):
    (occ, vir), (occ_to, vir_to) = source, target
    spans = (
        (occ % 4 - occ_to % 4, 4),
        (occ // 4 % 2 * 4 + vir // 2 - occ_to // 4 % 2 * 4 - vir_to // 2, 8),
        (occ // 8 - occ_to // 8, 12),
    )
    return sum(min(span % ring, -span % ring) for span, ring in spans)


def matched(costs, limit):
    held = [None] * 24

    def placed(block, seen):
        for place in sorted(range(24), key=lambda place: costs[block][place]):
            if costs[block][place] <= limit and place not in seen:
                seen.add(place)
                if held[place] is None or placed(held[place], seen):
                    held[place] = block
                    return True
        return False

    return held if all(placed(block, set()) for block in range(24)) else None


def owners():
    pairs, table = [], []
    for x in range(4):
        for v in range(8):
            blocks = [(v * 12 + x * 3 + block // 8, block % 8) for block in range(24)]
            costs = [[hops(block, (place * 4 + x, v)) for place in range(24)] for block in blocks]
            held = next(found for found in (matched(costs, limit) for limit in range(20)) if found)
            for first, second in list(itertools.combinations(range(24), 2)) * 6:
                one, two = held[first], held[second]
                if costs[one][first] ** 4 + costs[two][second] ** 4 > costs[one][second] ** 4 + costs[two][first] ** 4:
                    held[first], held[second] = two, one
            for place, block in enumerate(held):
                pairs.append((blocks[block][0] * 8 + blocks[block][1], (place * 4 + x) * 8 + v))
            table += [held.index(block) for block in range(24)]
    return pairs, table


def local(amplitudes, integrals, irrep_occ, irrep_j, irrep_vir, irrep_b):
    vir, b = irrep_vir.reshape(2, LANES), irrep_b.reshape(1, LANES)
    pairs, table = owners()
    table = jnp.asarray(table, jnp.int32)
    labels = (irrep_occ, irrep_j, vir, b)

    def owned(round_index):
        return lax.ppermute(pack(round_index, *labels, integrals)[0], AXES, pairs)

    def column(packed):
        copies = jnp.broadcast_to(packed[None], (24, SLAB, LANES))
        gathered = lax.all_to_all(copies, HOPS, split_axis=0, concat_axis=0, tiled=True)
        return gathered

    packed, rounds = pack(jnp.zeros((1,), jnp.int32), *labels, integrals)
    packed, amplitudes = lax.optimization_barrier((packed, amplitudes))
    packed = lax.ppermute(packed, AXES, pairs)
    x = lax.axis_index("x")

    def piece(shift):
        return lax.dynamic_slice_in_dim(amplitudes[0], lax.rem(x + shift, 4) * 4, 4)

    def exchanged(piece, shift):
        return lax.ppermute(piece, "x", [(s, (s + shift) % 4) for s in range(4)])

    rank, right, *opposite = prepare(vir, b, exchanged(piece(2), 2))
    known = (irrep_occ, irrep_j, rank, right)
    packed, *near = lax.optimization_barrier((packed, piece(0), piece(1), piece(3)))
    t = [near[0], exchanged(near[1], 1), exchanged(near[2], 3), *opposite]
    sums = multiply(table, jnp.zeros((1,), jnp.int32), *known, column(packed), t)

    def another(state):
        index, sums = state
        return index + 1, multiply(table, index[None], *known, column(owned(index[None])), t, sums)

    _, (own, given) = lax.while_loop(lambda state: state[0] < rounds[0], another, (jnp.int32(1), sums))
    total = own + lax.ppermute(given, "core", [(0, 1), (1, 0)])
    parts = lax.all_to_all(total, PLANE, split_axis=0, concat_axis=0, tiled=True)
    return jnp.sum(parts, axis=0, keepdims=True)


def solution(mesh):
    parts = Mesh(mesh.devices.reshape(12, 2, 4, 4, 2), AXES)
    occ, vir = ("z", "y_hi", "x"), ("y_lo", "core")
    return jax.shard_map(
        local,
        mesh=parts,
        in_specs=(P(occ, vir, None, None), P(occ, vir, None), P(), P(), P(), P()),
        out_specs=P(occ, None, vir, None),
        check_vma=False,
    )
```
